512 devices in a mesh: seq: 64 (over z, x, core), head: 8 (over y).
Axes of the slice: x: 4, y: 8, z: 8, core: 2. Of those that a mesh axis runs over, the one named last changes fastest.
Arguments:
- queries: bfloat16 [16384, 2048], P('seq', 'head'), may hold values from -40 to 40
- keys: bfloat16 [16384, 2048], P('seq', 'head'), may hold values from -40 to 40
- values: bfloat16 [16384, 2048], P('seq', 'head'), may hold values from -6 to 6
- text_keys: bfloat16 [256, 2048], P('seq', 'head'), may hold values from -6 to 6
- text_values: bfloat16 [256, 2048], P('seq', 'head'), may hold values from -6 to 6
- text_len: int32 [1], replicated, may hold values from 64 to 256
- radial_width: int32 [64, 5], replicated, may hold values from 32 to 256
- far_blocks: int32 [128, 29], replicated, may hold values from 0 to 127, as said below
- far_count: int32 [128], replicated, may hold values from 0 to 29
- w_out: bfloat16 [2048, 3072], P('head'), may hold values from -0.1875 to 0.1875
Outputs:
- mixed: bfloat16 [16384, 3072], P('seq', 'head')
The draws below stay inside these ranges and needn't reach their ends.
Inputs may be any that keep to these rules, and one draw needn't show every extreme that they name: `far_blocks`: within the rows of one frame group's query blocks, every listed block comes from a different frame group, and none from a group g with |g - own group| <= 2; so a group asks at most one block of any other group.
All inputs are finite; a program needn't handle non-finite values.
Results may differ from the reference program's by a relative error of at most 0.0057.
Values may be sent and summed in bfloat16 or wider, within the bound.
No kernel may reach another device: no remote copies, remote signals or barrier semaphores. Data moves between devices by JAX's collectives and lax.ppermute only.
A program may use at most 128 MiB of HBM per device.

```python
import jax
import jax.numpy as jnp
from jax import lax

D = 3072
HD = 128
HEADS = 16
TOK_DEV = 256
BLK = 128
NEAR = 2
TEXT = 256
GROUPS = 64
TOKENS = 16384
QB_DEV = 2
QUERY_TILE_COUNT = 128
FAR_MAX = 29


def draw_queries(key, part):
    key = jax.random.fold_in(key, 3)
    drawn = jax.random.truncated_normal(key, -4.0, 4.0, (TOKENS, HEADS * HD), jnp.float32)
    return drawn.astype(jnp.bfloat16)


def draw_keys(key, part):
    key = jax.random.fold_in(key, 4)
    drawn = jax.random.truncated_normal(key, -4.0, 4.0, (TOKENS, HEADS * HD), jnp.float32)
    return drawn.astype(jnp.bfloat16)


def draw_radial_width(key, part):
    key = jax.random.fold_in(key, 5)
    entries = GROUPS * (2 * NEAR + 1)
    flat = jax.random.randint(key, (entries,), TOK_DEV // 8, TOK_DEV + 1, jnp.int32)
    where_top = jax.random.randint(jax.random.fold_in(key, 1), (), 0, entries, jnp.int32)
    flat = flat.at[where_top].set(TOK_DEV)
    flat = flat.at[(where_top + 1) % entries].set(TOK_DEV // 8)
    return flat.reshape(GROUPS, 2 * NEAR + 1)


def draw_far_blocks(key, part):
    key = jax.random.fold_in(key, 7)
    group_ids = jnp.arange(GROUPS, dtype=jnp.int32)
    random_scores = jax.random.randint(key, (GROUPS, GROUPS), 0, 1 << 20, jnp.int32)
    distinct = random_scores * GROUPS + group_ids[None, :]
    excluded = jnp.abs(group_ids[None, :] - group_ids[:, None]) <= NEAR
    distinct = jnp.where(excluded, jnp.int32((1 << 20) * GROUPS + GROUPS), distinct)
    forced = (group_ids[:, None] == 0) & (group_ids[None, :] == GROUPS - 1) | (group_ids[:, None] == GROUPS - 1) & (group_ids[None, :] == 0)
    distinct = jnp.where(forced, jnp.int32(-1), distinct)
    ordering = jnp.argsort(distinct, axis=1).astype(jnp.int32)
    sources = ordering[:, :QB_DEV * FAR_MAX]
    within = jax.random.randint(jax.random.fold_in(key, 1), (GROUPS, QB_DEV * FAR_MAX), 0, QB_DEV, jnp.int32)
    return (sources * QB_DEV + within).reshape(QUERY_TILE_COUNT, FAR_MAX)


def draw_far_count(key, part):
    key = jax.random.fold_in(key, 9)
    level = jax.random.randint(key, (GROUPS, 1), 0, FAR_MAX + 1, jnp.int32)
    jitter = jax.random.randint(jax.random.fold_in(key, 1), (GROUPS, QB_DEV), -1, 2, jnp.int32)
    counts = jnp.clip(level + jitter, 0, FAR_MAX).reshape(QUERY_TILE_COUNT)
    where_top = jax.random.randint(jax.random.fold_in(key, 2), (), 0, QUERY_TILE_COUNT, jnp.int32)
    counts = counts.at[where_top].set(FAR_MAX)
    counts = counts.at[0].set(FAR_MAX)
    return counts.at[(GROUPS - 1) * QB_DEV].set(FAR_MAX)


def with_spikes(array, stream_key, source, target, shards_of, factor):
    def block_of(position):
        return (jnp.arange(array.shape[position]) // (array.shape[position] // shards_of)).reshape((-1,) + (1,) * (array.ndim - 1 - position))

    first = jax.random.permutation(stream_key, shards_of)[block_of(target)]
    second = (block_of(target) + shards_of // 2) % shards_of
    return jnp.where((block_of(source) == first) | (block_of(source) == second), factor * array, array)


def level_of(rng, shape, split, least, top_value):
    def one(position, shards_of):
        steps = jax.random.uniform(jax.random.fold_in(jax.random.fold_in(rng, 6), position), (shards_of,), jnp.float32, least / len(split), top_value / len(split))
        return jnp.repeat(jnp.exp(steps), shape[position] // shards_of).reshape((-1,) + (1,) * (len(shape) - position - 1))

    level = one(*split[0])
    for cut in split[1:]:
        level = level * one(*cut)
    return level


def bell_draw(key, dims, spread, bound, cuts=(), kind=jnp.bfloat16):
    values = jax.random.normal(key, dims, jnp.float32) * spread
    if len(cuts) > 0:
        values = level_of(key, dims, cuts, -0.22, 0.18) * values
    return jnp.clip(values, min=-bound, max=bound).astype(kind)


def gaussian_with(rng, extent, scale, most, shards, heavy, held_as=jnp.bfloat16):
    values = scale * jax.random.normal(rng, extent, jnp.float32)
    if shards:
        values = values * level_of(rng, extent, shards, -0.22, 0.18)
    return jnp.clip(with_spikes(values, jax.random.fold_in(rng, 3), *heavy), -most, most).astype(held_as)


def setup_inputs(seed: int = 0) -> dict:
    splits = jax.random.split(jax.random.key(seed), 11)
    queries = draw_queries(jax.random.fold_in(splits[10], 71), 0)
    keys = draw_keys(jax.random.fold_in(splits[10], 71), 0)
    values = bell_draw(splits[2], (TOKENS, HEADS * HD), 1.0, 6.0, ((0, 64), (1, 8)))
    text_keys = bell_draw(splits[3], (TEXT, HEADS * HD), 1.0, 6.0, ((0, 64), (1, 8)))
    text_values = bell_draw(splits[4], (TEXT, HEADS * HD), 1.0, 6.0, ((0, 64), (1, 8)))
    text_len = jax.random.randint(splits[5], (1,), TEXT // 4, TEXT + 1).astype(jnp.int32)
    radial_width = draw_radial_width(jax.random.fold_in(splits[10], 71), 0)
    far_blocks = draw_far_blocks(jax.random.fold_in(splits[10], 71), 0)
    far_count = draw_far_count(jax.random.fold_in(splits[10], 71), 0)
    w_out = gaussian_with(splits[9], (HEADS * HD, D), (HEADS * HD) ** -0.5, 0.1875, ((0, 8),), (0, 1, 8, 2.0))
    return {"queries": queries, "keys": keys, "values": values, "text_keys": text_keys, "text_values": text_values, "text_len": text_len, "radial_width": radial_width, "far_blocks": far_blocks, "far_count": far_count, "w_out": w_out}


def reference(queries, keys, values, text_keys, text_values, text_len, radial_width, far_blocks, far_count, w_out):
    width_all = HEADS * HD
    score_scale = HD ** -0.5
    margin = NEAR * TOK_DEV
    padded_keys = jnp.pad(keys, ((margin, margin), (0, 0)))
    padded_values = jnp.pad(values, ((margin, margin), (0, 0)))
    text_live = jnp.arange(TEXT, dtype=jnp.int32) < text_len[0]
    text_kf = text_keys.astype(jnp.float32).reshape(TEXT, HEADS, HD)
    text_vf = text_values.astype(jnp.float32).reshape(TEXT, HEADS, HD)
    offsets = jnp.arange(2 * NEAR + 1, dtype=jnp.int32) - NEAR
    key_positions = jnp.arange(TOK_DEV, dtype=jnp.int32)
    blocks_group = TOK_DEV // BLK

    def one_block(block_index):
        group = block_index // blocks_group
        query_positions = (block_index % blocks_group) * BLK + jnp.arange(BLK, dtype=jnp.int32)
        query_rows = lax.dynamic_slice_in_dim(queries, (block_index * BLK).astype(jnp.int32), BLK, 0)
        query_rows = query_rows.astype(jnp.float32).reshape(BLK, HEADS, HD)
        window_start = (group * TOK_DEV).astype(jnp.int32)
        near_keys = lax.dynamic_slice_in_dim(padded_keys, window_start, (2 * NEAR + 1) * TOK_DEV, 0)
        near_values = lax.dynamic_slice_in_dim(padded_values, window_start, (2 * NEAR + 1) * TOK_DEV, 0)
        widths = radial_width[group]
        present = (group + offsets >= 0) & (group + offsets < GROUPS)
        band_mask = (jnp.abs(query_positions[:, None, None] - key_positions[None, None, :]) < widths[None, :, None]) & present[None, :, None]
        band_mask = band_mask.reshape(BLK, (2 * NEAR + 1) * TOK_DEV)
        listed = far_blocks[block_index]
        listed_live = jnp.arange(FAR_MAX, dtype=jnp.int32) < far_count[block_index]
        row_index = (listed[:, None] * BLK + jnp.arange(BLK, dtype=jnp.int32)[None, :]).reshape(FAR_MAX * BLK)
        far_keys = jnp.take(keys, row_index, axis=0)
        far_values = jnp.take(values, row_index, axis=0)
        far_live = jnp.repeat(listed_live, BLK)
        all_keys = jnp.concatenate((text_kf, near_keys.astype(jnp.float32).reshape(-1, HEADS, HD), far_keys.astype(jnp.float32).reshape(-1, HEADS, HD)), axis=0)
        all_values = jnp.concatenate((text_vf, near_values.astype(jnp.float32).reshape(-1, HEADS, HD), far_values.astype(jnp.float32).reshape(-1, HEADS, HD)), axis=0)
        full_mask = jnp.concatenate((jnp.broadcast_to(text_live[None, :], (BLK, TEXT)), band_mask, jnp.broadcast_to(far_live[None, :], (BLK, FAR_MAX * BLK))), axis=1)
        logit_matrix = jnp.einsum("qhd,khd->hqk", query_rows, all_keys) * score_scale
        masked = jnp.where(full_mask[None], logit_matrix, -jnp.inf)
        highest = jnp.max(masked, axis=2, keepdims=True)
        exponent = jnp.where(full_mask[None], jnp.exp(masked - highest), jnp.float32(0.0))
        softmax_denominators = jnp.sum(exponent, axis=2, keepdims=True)
        rounded = lax.optimization_barrier(exponent.astype(jnp.bfloat16))
        summed = jnp.einsum("hqk,khd->hqd", rounded.astype(jnp.float32), all_values)
        result = (summed / softmax_denominators).astype(jnp.bfloat16)
        return jnp.transpose(result, (1, 0, 2)).reshape(BLK, width_all)

    attention = lax.map(one_block, jnp.arange(QUERY_TILE_COUNT, dtype=jnp.int32)).reshape(TOKENS, width_all)
    return jnp.dot(attention, w_out, preferred_element_type=jnp.float32).astype(jnp.bfloat16)
```

```python
import functools

import jax
import jax.numpy as jnp
from jax import lax
from jax.experimental import pallas as pl
from jax.experimental.pallas import tpu as pltpu
from jax.sharding import PartitionSpec as P

HD = 128
BLK = 128
NEAR = 2
ROW = 8
TPAD = 16
FAR_WIDTH = 1024
NEG = -1e30
FLOOR = -1e9
SCORE_SCALE = HD ** (-0.5) * 1.4426950408889634
EARLY = 5
EARLY_CHUNK = 4
LATE = 3
LATE_CHUNK = 2
STRIDE = 32
EARLY_AT = 2
LATE_AT = 24
HEADER = 2 * ROW * STRIDE


def row_peers():
    return [[z * ROW + r for r in range(ROW)] for z in range(ROW)]


def along_column(block, distance):
    count = ROW * ROW
    return lax.ppermute(block, "seq", [(g, (g + ROW * distance) % count) for g in range(count)])


def list_kernel(far_ref, count_ref, width_ref, len_ref, where_ref, table_ref):
    z = where_ref[0]
    r = where_ref[1]
    table_ref[HEADER] = z
    table_ref[HEADER + 1] = r
    table_ref[HEADER + 2] = len_ref[0]

    def one_group(q, _):
        group = z * ROW + q
        for a in range(2):
            qb = group * 2 + a
            base = (2 * q + a) * STRIDE
            live = count_ref[qb]
            n = jnp.int32(0)
            k = jnp.int32(0)
            for d in range(2 * NEAR + 1):
                h = group + d - NEAR
                inside = (h >= 0) & (h < ROW * ROW) & ((h & (ROW - 1)) == r)
                ahead = ((h >> 3) - z) & (ROW - 1)
                place = jnp.where(ahead == 0, 0, jnp.where(ahead == 1, 4, 2))
                code = width_ref[d, group] * 16 + place
                table_ref[base + EARLY_AT + n] = code
                table_ref[base + EARLY_AT + 1 + n] = code + 1
                n = n + jnp.where(inside, 2, 0)
            for m in range(far_ref.shape[0]):
                block = far_ref[m, qb]
                h = block >> 1
                inside = ((h & (ROW - 1)) == r) & (m < live)
                ahead = ((h >> 3) - z) & (ROW - 1)
                slot = jnp.where(ahead < ROW // 2, 2 * ahead, 2 * (ROW - ahead) - 1)
                slot = jnp.where(ahead == ROW // 2, ROW - 1, slot)
                early = inside & (slot < EARLY)
                late = inside & (slot >= EARLY)
                code = FAR_WIDTH * 16 + slot * 2 + (block & 1)
                table_ref[base + EARLY_AT + n] = code
                table_ref[base + LATE_AT + k] = code - 2 * EARLY
                n = jnp.minimum(n + jnp.where(early, 1, 0), LATE_AT - EARLY_AT - 2)
                k = jnp.minimum(k + jnp.where(late, 1, 0), STRIDE - LATE_AT - 1)
            table_ref[base] = n
            table_ref[base + 1] = k
        return 0

    lax.fori_loop(0, ROW, one_group, 0)


def rounded_top(top):
    high = top.astype(jnp.bfloat16).astype(jnp.float32)
    low = (top - high).astype(jnp.bfloat16).astype(jnp.float32)
    return high, low


def attend(table, late, q_ref, kv, text_bias, text_k, text_v, per_chunk, first_state, finish):
    rows = lax.broadcasted_iota(jnp.int32, (BLK, BLK), 0)
    cols = lax.broadcasted_iota(jnp.int32, (BLK, BLK), 1)
    offset = rows - cols

    def one_group(g, _):
        def chunk(c, states, with_text):
            work = []
            for a in range(2):
                base = (2 * g + a) * STRIDE
                items = []
                for j in range(per_chunk):
                    number = c * per_chunk + j
                    code = table[base + (LATE_AT if late else EARLY_AT) + number]
                    code = jnp.where(number < table[base + late], code, 0)
                    side = code & 1
                    live = jnp.abs(offset + (side - a) * BLK) < (code >> 4)
                    items.append(((code & 15) >> 1, pl.multiple_of(side * BLK, BLK), live))
                for h in range(2):
                    lanes = slice(h * HD, (h + 1) * HD)
                    query = q_ref[g, a * BLK : (a + 1) * BLK, lanes]
                    key_rows = [kv[w, pl.ds(s, BLK), lanes] for w, s, _ in items]
                    value_cols = [kv[w, pl.ds(s + 2 * BLK, BLK), lanes] for w, s, _ in items]
                    if with_text:
                        key_rows.append(text_k[:, lanes])
                        value_cols.append(text_v[h])
                    product = lax.dot_general(
                        jnp.concatenate(key_rows, axis=0),
                        query,
                        (((1,), (1,)), ((), ())),
                        preferred_element_type=jnp.float32,
                    )
                    work.append((product, value_cols, items))
            fresh = []
            for x, (product, value_cols, items) in enumerate(work):
                parts = []
                for j, (_, _, live) in enumerate(items):
                    s = product[j * BLK : (j + 1) * BLK] * SCORE_SCALE
                    parts.append(jnp.where(live, s, NEG))
                if with_text:
                    parts.append(product[per_chunk * BLK :] * SCORE_SCALE + text_bias[...])
                old_top, old_total, old_acc = states[x] if states is not None else (FLOOR, None, None)
                peak = [jnp.max(s, axis=0, keepdims=True) for s in parts]
                top = jnp.maximum(functools.reduce(jnp.maximum, peak), old_top)
                high, low = rounded_top(top)
                top = high + low
                weights = [jnp.exp2(s - top) for s in parts]
                total = functools.reduce(jnp.add, [jnp.sum(p, axis=0, keepdims=True) for p in weights])
                acc = jnp.dot(
                    jnp.concatenate(value_cols, axis=1),
                    jnp.concatenate([p.astype(jnp.bfloat16) for p in weights], axis=0),
                    preferred_element_type=jnp.float32,
                )
                if states is not None:
                    fade = jnp.exp2(old_top - top)
                    total = total + old_total * fade
                    acc = acc + old_acc * fade
                fresh.append((top, total, acc))
            return tuple(fresh)

        states = chunk(0, first_state(g), True)
        most = jnp.maximum(table[2 * g * STRIDE + late], table[(2 * g + 1) * STRIDE + late])
        states = lax.fori_loop(
            1, (most + per_chunk - 1) // per_chunk, lambda c, s: chunk(c, s, False), states
        )
        for a in range(2):
            finish(g, a, states[2 * a], states[2 * a + 1])
        return 0

    lax.fori_loop(0, ROW, one_group, 0)


def set_text(kv, slot_rows, text_len, text_bias, text_k, text_v):
    count = len(slot_rows)
    rows = lax.broadcasted_iota(jnp.int32, (TPAD, BLK), 0)
    for s, first in enumerate(slot_rows):
        alive = (rows < 4) & (first + rows < text_len)
        text_bias[s * TPAD : (s + 1) * TPAD, :] = jnp.where(alive, 0.0, NEG)
    text_k[...] = kv[:, 4 * BLK : 4 * BLK + TPAD, :].reshape(count * TPAD, 2 * HD)
    raw = kv[:, 4 * BLK + TPAD : 4 * BLK + 2 * TPAD, :].reshape(count * TPAD, 2 * HD)
    for h in range(2):
        text_v[h] = raw[:, h * HD : (h + 1) * HD].astype(jnp.float32).T.astype(jnp.bfloat16)


def text_rows(table, steps):
    z = table[HEADER]
    r = table[HEADER + 1]
    return [(((z + d + ROW) % ROW) * ROW + r) * 4 for d in steps]


def early_kernel(
    table, q_ref, own, f1, b1, f2, b2, acc_ref, stat_ref,
    kv, sems, text_bias, text_k, text_v,
):
    copies = [
        pltpu.make_async_copy(src, kv.at[i], sems.at[i]) for i, src in enumerate((own, f1, b1, f2, b2))
    ]
    for copy in copies:
        copy.start()
    for copy in copies:
        copy.wait()
    rows = text_rows(table, (0, -1, 1, -2, 2))
    set_text(kv, rows, table[HEADER + 2], text_bias, text_k, text_v)

    def finish(g, a, *heads):
        lanes = slice(a * BLK, (a + 1) * BLK)
        stats = []
        for h, (top, total, acc) in enumerate(heads):
            acc_ref[g, h * HD : (h + 1) * HD, lanes] = acc
            stats += [top, total]
        stats.append(jnp.zeros((4, BLK), jnp.float32))
        stat_ref[g, :, lanes] = jnp.concatenate(stats, axis=0)

    attend(
        table, 0, q_ref, kv, text_bias, text_k, text_v, EARLY_CHUNK, lambda g: None, finish
    )


def late_kernel(
    table, q_ref, f3, b3, f4, b4, acc_ref, stat_ref, out_ref,
    kv, sems, text_bias, text_k, text_v,
):
    copies = [
        pltpu.make_async_copy(f3, kv.at[0], sems.at[0]),
        pltpu.make_async_copy(b3, kv.at[1], sems.at[1]),
        pltpu.make_async_copy(f4, kv.at[2, : 2 * BLK], sems.at[2]),
        pltpu.make_async_copy(b4, kv.at[2, 2 * BLK :], sems.at[3]),
    ]
    for copy in copies:
        copy.start()
    for copy in copies:
        copy.wait()
    rows = text_rows(table, (-3, 3, 4))
    set_text(kv, rows, table[HEADER + 2], text_bias, text_k, text_v)

    def first_state(g):
        states = []
        for a in range(2):
            lanes = slice(a * BLK, (a + 1) * BLK)
            for h in range(2):
                states.append(
                    (
                        stat_ref[g, 2 * h : 2 * h + 1, lanes],
                        stat_ref[g, 2 * h + 1 : 2 * h + 2, lanes],
                        acc_ref[g, h * HD : (h + 1) * HD, lanes],
                    )
                )
        return states

    def finish(g, a, *heads):
        lanes = slice(a * BLK, (a + 1) * BLK)
        stats = []
        for h, (top, total, acc) in enumerate(heads):
            out_ref[g, h * HD : (h + 1) * HD, lanes] = acc.astype(jnp.bfloat16)
            stats += list(rounded_top(top)) + list(rounded_top(total))
        stats.append(jnp.zeros((TPAD - len(stats), BLK), jnp.float32))
        out_ref[g, 2 * HD : 2 * HD + TPAD, lanes] = jnp.concatenate(stats, axis=0).astype(jnp.bfloat16)

    attend(
        table, 1, q_ref, kv, text_bias, text_k, text_v, LATE_CHUNK, first_state, finish
    )


def merge_kernel(part_ref, out_ref):
    stats = [part_ref[i, 2 * HD : 2 * HD + TPAD, :].astype(jnp.float32) for i in range(ROW)]
    for h in range(2):
        tops = [s[4 * h : 4 * h + 1] + s[4 * h + 1 : 4 * h + 2] for s in stats]
        sums = [s[4 * h + 2 : 4 * h + 3] + s[4 * h + 3 : 4 * h + 4] for s in stats]
        top = functools.reduce(jnp.maximum, tops)
        weights = [jnp.exp2(t - top) for t in tops]
        total = functools.reduce(jnp.add, [w * s for w, s in zip(weights, sums)])
        inverse = 1.0 / total
        rows = slice(h * HD, (h + 1) * HD)
        acc = None
        for i in range(ROW):
            term = part_ref[i, rows, :].astype(jnp.float32) * weights[i]
            acc = term if acc is None else acc + term
        acc = (acc * inverse).astype(jnp.bfloat16)
        for i in range(ROW):
            out_ref[i, rows, :] = acc


def smem():
    return pl.BlockSpec(memory_space=pltpu.SMEM)


def vmem():
    return pl.BlockSpec(memory_space=pltpu.VMEM)


def anywhere():
    return pl.BlockSpec(memory_space=pl.ANY)


def kernel_params():
    return pltpu.CompilerParams(vmem_limit_bytes=32 << 20)


def attend_scratch(slots, copies):
    return [
        pltpu.VMEM((slots, 4 * BLK + 2 * TPAD, 2 * HD), jnp.bfloat16),
        pltpu.SemaphoreType.DMA((copies,)),
        pltpu.VMEM((slots * TPAD, BLK), jnp.float32),
        pltpu.VMEM((slots * TPAD, 2 * HD), jnp.bfloat16),
        pltpu.VMEM((2, HD, slots * TPAD), jnp.bfloat16),
    ]


def shards(
    queries,
    keys,
    values,
    text_keys,
    text_values,
    text_len,
    radial_width,
    far_blocks,
    far_count,
    w_out,
):
    own = lax.axis_index("seq")
    where = jnp.stack((own // ROW, own % ROW)).astype(jnp.int32)
    tokens, width = queries.shape
    heads = lax.axis_size("head")
    columns = w_out.shape[1] // heads

    turned = values.reshape(2, BLK, 2, HD).transpose(0, 3, 2, 1).reshape(tokens, width)
    pad = ((0, TPAD - text_keys.shape[0]), (0, 0))
    kv = jnp.concatenate((keys, turned, jnp.pad(text_keys, pad), jnp.pad(text_values, pad)), axis=0)
    f1 = along_column(kv, 1)
    b1 = along_column(kv, -1)
    q_all = lax.all_to_all(
        jnp.broadcast_to(queries[None], (ROW, tokens, width)), "seq", 0, 0, axis_index_groups=row_peers()
    )
    f2 = along_column(f1, 1)
    b2 = along_column(b1, -1)
    f3 = along_column(f2, 1)
    b3 = along_column(b2, -1)
    f4 = along_column(f2[: 2 * BLK], 2)
    b4 = along_column(b2[2 * BLK :], -2)

    half = lax.dynamic_slice_in_dim(w_out, (own % 2) * HD, HD, 0)
    half = half.reshape(HD, heads, columns).transpose(1, 0, 2)
    half, q_all = lax.optimization_barrier((half, q_all))
    half = lax.all_to_all(half, "head", 0, 0)
    other = lax.ppermute(half, "seq", [(g, g ^ 1) for g in range(ROW * ROW)])

    table = pl.pallas_call(
        list_kernel,
        out_shape=jax.ShapeDtypeStruct((HEADER + 8,), jnp.int32),
        in_specs=[smem()] * 5,
        out_specs=smem(),
        cost_estimate=pl.CostEstimate(flops=2 * 10**9, bytes_accessed=10**5, transcendentals=0),
        name="lists",
    )(far_blocks.T, far_count, radial_width.T, text_len, where)

    acc, stat = pl.pallas_call(
        early_kernel,
        out_shape=(
            jax.ShapeDtypeStruct((ROW, width, tokens), jnp.float32),
            jax.ShapeDtypeStruct((ROW, 8, tokens), jnp.float32),
        ),
        in_specs=[smem(), vmem()] + [anywhere()] * 5,
        out_specs=(vmem(), vmem()),
        scratch_shapes=attend_scratch(EARLY, 5),
        compiler_params=kernel_params(),
        cost_estimate=pl.CostEstimate(flops=8 * 10**9, bytes_accessed=5 * 10**6, transcendentals=0),
        name="attend_early",
    )(table, q_all, kv, f1, b1, f2, b2)
    part = pl.pallas_call(
        late_kernel,
        out_shape=jax.ShapeDtypeStruct((ROW, width + TPAD, tokens), jnp.bfloat16),
        in_specs=[smem(), vmem()] + [anywhere()] * 4 + [vmem()] * 2,
        out_specs=vmem(),
        scratch_shapes=attend_scratch(LATE, 4),
        compiler_params=kernel_params(),
        cost_estimate=pl.CostEstimate(flops=7 * 10**9, bytes_accessed=5 * 10**6, transcendentals=0),
        name="attend_late",
    )(table, q_all, f3, b3, f4, b4, acc, stat)
    part, half = lax.optimization_barrier((part, half))
    part = lax.all_to_all(part, "seq", 0, 0, axis_index_groups=row_peers())
    merged = pl.pallas_call(
        merge_kernel,
        out_shape=jax.ShapeDtypeStruct((ROW, width, tokens), jnp.bfloat16),
        in_specs=[vmem()],
        out_specs=vmem(),
        compiler_params=kernel_params(),
        name="merge",
    )(part)
    attention = lax.all_to_all(merged, "head", 0, 0)
    even = own % 2 == 0
    w_mine = jnp.concatenate((jnp.where(even, half, other), jnp.where(even, other, half)), axis=1)
    mixed = lax.dot_general(
        attention.reshape(heads * width, tokens),
        w_mine.reshape(heads * width, columns),
        (((0,), (0,)), ((), ())),
        preferred_element_type=jnp.float32,
    )
    return mixed.astype(jnp.bfloat16)


def solution(mesh):
    return jax.shard_map(
        shards,
        mesh=mesh,
        in_specs=(
            P("seq", "head"),
            P("seq", "head"),
            P("seq", "head"),
            P("seq", "head"),
            P("seq", "head"),
            P(),
            P(),
            P(),
            P(),
            P("head", None),
        ),
        out_specs=P("seq", "head"),
        check_vma=False,
    )
```

```python
import functools

import jax
import jax.numpy as jnp
from jax import lax
from jax.experimental import pallas as pl
from jax.experimental.pallas import tpu as pltpu
from jax.sharding import PartitionSpec as P

HD = 128
BLK = 128
NEAR = 2
ROW = 8
TPAD = 16
NEG = -1e30
FLOOR = -1e9
SCORE_SCALE = HD ** (-0.5) * 1.4426950408889634
EARLY = (0, -1, 1, -2, 2)
LATE = (-3, 3, 4)
TOGETHER = 4
TEXT_ROWS = 8
GROUPS_AT_ONCE = 4
MESSAGE = 4 * BLK + TPAD
NEAR_AT = ROW
LEN_AT = ROW + 1
WHERE_AT = ROW + 2


def row_peers():
    return [[z * ROW + r for r in range(ROW)] for z in range(ROW)]


def along_column(block, distance):
    count = ROW * ROW
    return lax.ppermute(block, "seq", [(g, (g + ROW * distance) % count) for g in range(count)])


def turned(buf):
    for a in range(2):
        for h in range(2):
            tile = buf[a * BLK : (a + 1) * BLK, h * HD : (h + 1) * HD].astype(jnp.float32)
            yield a, h, tile.T.astype(jnp.bfloat16)


def key_kernel(k_in, v_in, text_in, kv_out, v_buf, sems):
    copies = [
        pltpu.make_async_copy(v_in, v_buf, sems.at[0]),
        pltpu.make_async_copy(k_in, kv_out.at[: 2 * BLK], sems.at[1]),
    ]
    for copy in copies:
        copy.start()
    kv_out[4 * BLK :, :] = text_in[...]
    copies[0].wait()
    for a, h, tile in turned(v_buf):
        kv_out[(2 + a) * BLK : (3 + a) * BLK, h * HD : (h + 1) * HD] = tile
    copies[1].wait()


def query_kernel(q_in, q_out, q_buf, sems):
    copy = pltpu.make_async_copy(q_in, q_buf, sems.at[0])
    copy.start()
    copy.wait()
    for a, h, tile in turned(q_buf):
        for i in range(ROW):
            q_out[i, a * BLK : (a + 1) * BLK, h * HD : (h + 1) * HD] = tile


def weight_kernel(where_ref, w_in, w_out, sems):
    heads, rows, columns = w_out.shape
    start = pl.multiple_of((where_ref[1] & 3) * rows, rows)
    copies = [
        pltpu.make_async_copy(
            w_in.at[pl.ds(start, rows), i * columns : (i + 1) * columns], w_out.at[i], sems.at[i]
        )
        for i in range(heads)
    ]
    for copy in copies:
        copy.start()
    for copy in copies:
        copy.wait()


def list_kernel(where_ref, far_ref, width_ref, table_ref):
    z = where_ref[0]
    r = where_ref[1]
    rows = 2 * ROW
    slots = far_ref.shape[1] - 1
    mine = far_ref[pl.ds(pl.multiple_of(z * rows, rows), rows), :]
    place = lax.broadcasted_iota(jnp.int32, mine.shape, 1)
    count = jnp.sum(jnp.where(place == slots, mine, 0), axis=1, keepdims=True)
    live = place < count
    live = live & (place < slots)
    lane = lax.broadcasted_iota(jnp.int32, (rows, BLK), 1)
    table = jnp.where(lane == LEN_AT, where_ref[2], 0)
    table = jnp.where(lane == WHERE_AT, z, table)
    table = jnp.where(lane == WHERE_AT + 1, r, table)
    for s, step in enumerate(EARLY + LATE):
        group = ((z + step) & (ROW - 1)) * ROW + r
        asked = jnp.where(live & ((mine >> 1) == group), 1 + (mine & 1), 0)
        table = jnp.where(lane == s, jnp.sum(asked, axis=1, keepdims=True), table)
    widths = width_ref[pl.ds(pl.multiple_of(z * ROW, ROW), ROW), :]
    place = lax.broadcasted_iota(jnp.int32, widths.shape, 1)
    query = lax.broadcasted_iota(jnp.int32, widths.shape, 0)
    offset = (r - query + NEAR) & (ROW - 1)
    group = z * ROW + query + offset - NEAR
    valid = (group >= 0) & (group < ROW * ROW) & (place == offset)
    step = (group >> 3) - z
    slot = jnp.where(step == 0, 0, jnp.where(step < 0, 1, 2))
    near = jnp.sum(jnp.where(valid, widths * 16 + slot, 0), axis=1, keepdims=True)
    near = jnp.concatenate((near, jnp.zeros((rows - ROW, 1), jnp.int32)), axis=0)
    table_ref[...] = jnp.where(lane == NEAR_AT, near, table)


def three_parts(x):
    high = x.astype(jnp.bfloat16).astype(jnp.float32)
    rest = x - high
    middle = rest.astype(jnp.bfloat16).astype(jnp.float32)
    return [high, middle, rest - middle]


def two_parts(x):
    high = x.astype(jnp.bfloat16).astype(jnp.float32)
    return [high, x - high]


def list_units(table, first, count, units):
    def one_block(i, n):
        for s in range(count):
            asked = table[i, first + s]
            units[n] = i * 16 + s * 2 + asked - 1
            n = n + jnp.where(asked > 0, 1, 0)
        return n

    return lax.fori_loop(0, 2 * ROW, one_block, jnp.int32(0))


def set_text(kv, table, steps, bias, text_k, text_v):
    z = table[0, WHERE_AT]
    r = table[0, WHERE_AT + 1]
    total = text_k.shape[0]
    row = lax.broadcasted_iota(jnp.int32, (TEXT_ROWS, 2 * BLK), 0)
    keys = []
    vals = []
    for s, step in enumerate(steps):
        first = (((z + step) & (ROW - 1)) * ROW + r) * 4
        alive = (row < 4) & (first + row < table[0, LEN_AT])
        bias[s * TEXT_ROWS : (s + 1) * TEXT_ROWS, :] = jnp.where(alive, 0.0, NEG)
        tile = kv[s, 4 * BLK : 4 * BLK + TPAD, :].astype(jnp.float32)[:TEXT_ROWS]
        keys.append(tile)
        vals.append(pltpu.roll(tile, 4, 0))
    spare = total - len(steps) * TEXT_ROWS
    bias[total - spare :, :] = jnp.full((spare, 2 * BLK), NEG, jnp.float32)
    keys.append(jnp.zeros((spare, 2 * HD), jnp.float32))
    text_k[...] = jnp.concatenate(keys, axis=0).astype(jnp.bfloat16)
    vals.append(jnp.zeros((HD - len(steps) * TEXT_ROWS, 2 * HD), jnp.float32))
    vals = jnp.concatenate(vals, axis=0)
    for h in range(2):
        text_v[h] = vals[:, h * HD : (h + 1) * HD].T.astype(jnp.bfloat16)


def group_queries(q_ref, g, h):
    lanes = slice(h * HD, (h + 1) * HD)
    return jnp.concatenate((q_ref[g, :BLK, lanes], q_ref[g, BLK:, lanes]), axis=1)


def product(left, right):
    return jnp.dot(left, right, preferred_element_type=jnp.float32)


def head_rows(h):
    return slice(h * HD, (h + 1) * HD)


def text_step(q_ref, cases, text_k, text_v, bias):
    spare = HD - text_k.shape[0]
    scores = [
        product(text_k[:, head_rows(h)], group_queries(q_ref, g, h)) * SCORE_SCALE + bias[...] for g, h in cases
    ]
    tops = [jnp.maximum(jnp.max(s, axis=0, keepdims=True), FLOOR) for s in scores]
    weights = [jnp.exp2(s - top) for s, top in zip(scores, tops)]
    totals = [jnp.sum(p, axis=0, keepdims=True) for p in weights]
    filler = jnp.zeros((spare, 2 * BLK), jnp.bfloat16)
    outs = [
        product(text_v[h], jnp.concatenate((p.astype(jnp.bfloat16), filler), axis=0))
        for (_, h), p in zip(cases, weights)
    ]
    return list(zip(tops, totals, outs))


def group_cases(step, groups):
    return [(step * groups + j, h) for j in range(groups) for h in range(2)]


def joined(old, new):
    top = jnp.maximum(old[0], new[0])
    fade = jnp.exp2(old[0] - top)
    rise = jnp.exp2(new[0] - top)
    return top, old[1] * fade + new[1] * rise, old[2] * fade + new[2] * rise


def read_state(acc, stat, g, h):
    return stat[g, 2 * h : 2 * h + 1, :], stat[g, 2 * h + 1 : 2 * h + 2, :], acc[g, head_rows(h), :]


def write_state(acc, stat, g, h, state):
    stat[g, 2 * h : 2 * h + 1, :] = state[0]
    stat[g, 2 * h + 1 : 2 * h + 2, :] = state[1]
    acc[g, head_rows(h), :] = state[2]


def walk_units(units, count, q_ref, kv, acc, stat):
    def step(t, _):
        work = []
        for j in range(TOGETHER):
            number = t * TOGETHER + j
            code = jnp.where(number < count, units[number], 0)
            gone = jnp.where(number < count, 0.0, NEG)
            block = code >> 4
            g = block >> 1
            across = pl.multiple_of((block & 1) * BLK, BLK)
            who = (code & 15) >> 1
            down = pl.multiple_of((code & 1) * BLK, BLK)
            for h in range(2):
                s = product(
                    kv[who, pl.ds(down, BLK), head_rows(h)], q_ref[g, pl.ds(across, BLK), head_rows(h)]
                )
                work.append((g, across, who, down, h, gone, s * SCORE_SCALE))
        done = []
        for g, across, who, down, h, gone, s in work:
            top = jnp.max(s, axis=0, keepdims=True)
            p = jnp.exp2(s - top)
            total = jnp.sum(p, axis=0, keepdims=True)
            out = product(kv[who, pl.ds(down + 2 * BLK, BLK), head_rows(h)], p.astype(jnp.bfloat16))
            done.append((g, across, h, top + gone, total, out))
        for g, across, h, top, total, out in done:
            lanes = pl.ds(across, BLK)
            old_top = stat[g, 2 * h : 2 * h + 1, lanes]
            new_top = jnp.maximum(old_top, top)
            fade = jnp.exp2(old_top - new_top)
            rise = jnp.exp2(top - new_top)
            stat[g, 2 * h : 2 * h + 1, lanes] = new_top
            stat[g, 2 * h + 1 : 2 * h + 2, lanes] = (
                stat[g, 2 * h + 1 : 2 * h + 2, lanes] * fade + total * rise
            )
            acc[g, head_rows(h), lanes] = acc[g, head_rows(h), lanes] * fade + out * rise
        return 0

    lax.fori_loop(0, (count + TOGETHER - 1) // TOGETHER, step, 0)


def wait_all(pairs, sems):
    copies = [pltpu.make_async_copy(src, dst, sems.at[i]) for i, (src, dst) in enumerate(pairs)]
    for copy in copies:
        copy.start()
    for copy in copies:
        copy.wait()


def early_kernel(
    table, q_in, own, f1, b1, f2, b2, acc, stat, q_ref, kv, units, sems, bias, text_k, text_v
):
    wait_all([(x, kv.at[i]) for i, x in enumerate((own, f1, b1, f2, b2))] + [(q_in, q_ref)], sems)
    set_text(kv, table, EARLY, bias, text_k, text_v)
    offset = lax.broadcasted_iota(jnp.int32, (2 * BLK, 2 * BLK), 0) - lax.broadcasted_iota(
        jnp.int32, (2 * BLK, 2 * BLK), 1
    )
    distance = jnp.abs(offset)

    def some_text(step, _):
        cases = group_cases(step, GROUPS_AT_ONCE)
        for (g, h), state in zip(cases, text_step(q_ref, cases, text_k, text_v, bias)):
            write_state(acc, stat, g, h, state)
        for g, h in cases[::2]:
            stat[g, 4:8, :] = jnp.zeros((4, 2 * BLK), jnp.float32)
        return 0

    lax.fori_loop(0, ROW // GROUPS_AT_ONCE, some_text, 0)

    def one_group(g, _):
        near = table[g, NEAR_AT]

        @pl.when(near > 0)
        def _():
            who = near & 15
            scores = []
            for h in range(2):
                s = product(kv[who, : 2 * BLK, head_rows(h)], group_queries(q_ref, g, h)) * SCORE_SCALE
                scores.append(jnp.where(distance < (near >> 4), s, NEG))
            fresh = []
            for h, s in enumerate(scores):
                top = jnp.max(s, axis=0, keepdims=True)
                p = jnp.exp2(s - top)
                values = jnp.concatenate(
                    (kv[who, 2 * BLK : 3 * BLK, head_rows(h)], kv[who, 3 * BLK : 4 * BLK, head_rows(h)]),
                    axis=1,
                )
                fresh.append((top, jnp.sum(p, axis=0, keepdims=True), product(values, p.astype(jnp.bfloat16))))
            for h, new in enumerate(fresh):
                write_state(acc, stat, g, h, joined(read_state(acc, stat, g, h), new))

        return 0

    lax.fori_loop(0, ROW, one_group, 0)
    walk_units(units, list_units(table, 0, len(EARLY), units), q_ref, kv, acc, stat)


def late_kernel(
    table, q_in, f3, b3, far4, acc_in, stat_in, out_ref,
    q_ref, kv, units, sems, bias, text_k, text_v, acc, stat,
):
    wait_all(
        [
            (f3, kv.at[0]),
            (b3, kv.at[1]),
            (far4, kv.at[2]),
            (q_in, q_ref),
            (acc_in, acc),
            (stat_in, stat),
        ],
        sems,
    )
    set_text(kv, table, LATE, bias, text_k, text_v)
    walk_units(units, list_units(table, len(EARLY), len(LATE), units), q_ref, kv, acc, stat)

    def some_groups(step, _):
        cases = group_cases(step, GROUPS_AT_ONCE)
        fresh = text_step(q_ref, cases, text_k, text_v, bias)
        done = [joined(read_state(acc, stat, g, h), new) for (g, h), new in zip(cases, fresh)]
        for x in range(0, len(cases), 2):
            g = cases[x][0]
            rows = []
            for h in range(2):
                top, total, out = done[x + h]
                out_ref[g, head_rows(h), :] = out.astype(jnp.bfloat16)
                rows += three_parts(top) + two_parts(total)
            rows.append(jnp.zeros((TPAD - len(rows), 2 * BLK), jnp.float32))
            out_ref[g, 2 * HD : 2 * HD + TPAD, :] = jnp.concatenate(rows, axis=0).astype(jnp.bfloat16)
        return 0

    lax.fori_loop(0, ROW // GROUPS_AT_ONCE, some_groups, 0)


def merge_kernel(part_ref, out_ref):
    stats = [part_ref[i, 2 * HD : 2 * HD + TPAD, :].astype(jnp.float32) for i in range(ROW)]
    for h in range(2):
        tops = [s[5 * h : 5 * h + 1] + s[5 * h + 1 : 5 * h + 2] + s[5 * h + 2 : 5 * h + 3] for s in stats]
        sums = [s[5 * h + 3 : 5 * h + 4] + s[5 * h + 4 : 5 * h + 5] for s in stats]
        top = functools.reduce(jnp.maximum, tops)
        weights = [jnp.exp2(t - top) for t in tops]
        total = functools.reduce(jnp.add, [w * s for w, s in zip(weights, sums)])
        inverse = 1.0 / total
        rows = slice(h * HD, (h + 1) * HD)
        acc = None
        for i in range(ROW):
            term = part_ref[i, rows, :].astype(jnp.float32) * weights[i]
            acc = term if acc is None else acc + term
        acc = (acc * inverse).astype(jnp.bfloat16)
        for i in range(ROW):
            out_ref[i, rows, :] = acc


def smem():
    return pl.BlockSpec(memory_space=pltpu.SMEM)


def vmem():
    return pl.BlockSpec(memory_space=pltpu.VMEM)


def anywhere():
    return pl.BlockSpec(memory_space=pl.ANY)


def kernel_params():
    return pltpu.CompilerParams(vmem_limit_bytes=32 << 20)


def attend_scratch(slots, copies, text_rows):
    return [
        pltpu.VMEM((ROW, 2 * BLK, 2 * HD), jnp.bfloat16),
        pltpu.VMEM((slots, MESSAGE, 2 * HD), jnp.bfloat16),
        pltpu.SMEM((2 * ROW * slots + 8,), jnp.int32),
        pltpu.SemaphoreType.DMA((copies,)),
        pltpu.VMEM((text_rows, 2 * BLK), jnp.float32),
        pltpu.VMEM((text_rows, 2 * HD), jnp.bfloat16),
        pltpu.VMEM((2, HD, HD), jnp.bfloat16),
    ]


def shards(
    queries,
    keys,
    values,
    text_keys,
    text_values,
    text_len,
    radial_width,
    far_blocks,
    far_count,
    w_out,
):
    own = lax.axis_index("seq")
    where = jnp.stack((own // ROW, own % ROW, text_len[0])).astype(jnp.int32)
    tokens, width = queries.shape
    heads = lax.axis_size("head")
    columns = w_out.shape[1] // heads

    text = jnp.concatenate(
        (text_keys, text_values, jnp.zeros((TPAD - 2 * text_keys.shape[0], width), jnp.bfloat16)), axis=0
    )
    whole = pltpu.CompilerParams(vmem_limit_bytes=60 << 20)
    kv = pl.pallas_call(
        key_kernel,
        out_shape=jax.ShapeDtypeStruct((MESSAGE, width), jnp.bfloat16),
        in_specs=[anywhere(), anywhere(), vmem()],
        out_specs=vmem(),
        scratch_shapes=[pltpu.VMEM((tokens, width), jnp.bfloat16), pltpu.SemaphoreType.DMA((2,))],
        compiler_params=whole,
        name="key_message",
    )(keys, values, text)
    kv, queries = lax.optimization_barrier((kv, queries))
    q_mine = pl.pallas_call(
        query_kernel,
        out_shape=jax.ShapeDtypeStruct((ROW, tokens, width), jnp.bfloat16),
        in_specs=[anywhere()],
        out_specs=vmem(),
        scratch_shapes=[pltpu.VMEM((tokens, width), jnp.bfloat16), pltpu.SemaphoreType.DMA((1,))],
        compiler_params=whole,
        name="query_message",
    )(queries)
    quarter = pl.pallas_call(
        weight_kernel,
        out_shape=jax.ShapeDtypeStruct((heads, width // 4, columns), jnp.bfloat16),
        in_specs=[smem(), anywhere()],
        out_specs=vmem(),
        scratch_shapes=[pltpu.SemaphoreType.DMA((heads,))],
        compiler_params=whole,
        name="weight_message",
    )(where, w_out)
    table = pl.pallas_call(
        list_kernel,
        out_shape=jax.ShapeDtypeStruct((2 * ROW, BLK), jnp.int32),
        in_specs=[smem(), vmem(), vmem()],
        out_specs=vmem(),
        cost_estimate=pl.CostEstimate(flops=10**9, bytes_accessed=10**5, transcendentals=0),
        name="lists",
    )(where, jnp.concatenate((far_blocks, far_count[:, None]), axis=1), radial_width)

    count = ROW * ROW
    f1 = along_column(kv, 1)
    b1 = along_column(kv, -1)
    q_all = lax.all_to_all(q_mine, "seq", 0, 0, axis_index_groups=row_peers())
    f2 = along_column(f1, 1)
    b2 = along_column(b1, -1)
    f2, b2, table, quarter = lax.optimization_barrier((f2, b2, table, quarter))
    f3 = along_column(f2, 1)
    b3 = along_column(b2, -1)
    far4 = lax.ppermute(
        jnp.where(own % 2 == 0, f2, b2),
        "seq",
        [(g, (g + (2 * ROW if g % 2 == 0 else -2 * ROW)) % count) for g in range(count)],
    )
    quarter, q_all = lax.optimization_barrier((quarter, q_all))
    quarter = lax.all_to_all(quarter, "head", 0, 0)

    acc, stat = pl.pallas_call(
        early_kernel,
        out_shape=(
            jax.ShapeDtypeStruct((ROW, width, tokens), jnp.float32),
            jax.ShapeDtypeStruct((ROW, 8, tokens), jnp.float32),
        ),
        in_specs=[smem()] + [anywhere()] * 6,
        out_specs=(vmem(), vmem()),
        scratch_shapes=attend_scratch(len(EARLY), 6, 48),
        compiler_params=kernel_params(),
        cost_estimate=pl.CostEstimate(flops=6 * 10**9, bytes_accessed=5 * 10**6, transcendentals=0),
        name="attend_early",
    )(table, q_all, kv, f1, b1, f2, b2)
    part = pl.pallas_call(
        late_kernel,
        out_shape=jax.ShapeDtypeStruct((ROW, width + TPAD, tokens), jnp.bfloat16),
        in_specs=[smem()] + [anywhere()] * 6,
        out_specs=vmem(),
        scratch_shapes=attend_scratch(len(LATE), 6, 32)
        + [pltpu.VMEM((ROW, width, tokens), jnp.float32), pltpu.VMEM((ROW, 8, tokens), jnp.float32)],
        compiler_params=kernel_params(),
        cost_estimate=pl.CostEstimate(flops=4 * 10**9, bytes_accessed=5 * 10**6, transcendentals=0),
        name="attend_late",
    )(table, q_all, f3, b3, far4, acc, stat)
    part, quarter = lax.optimization_barrier((part, quarter))
    part = lax.all_to_all(part, "seq", 0, 0, axis_index_groups=row_peers())
    part, quarter = lax.optimization_barrier((part, quarter))
    merged = pl.pallas_call(
        merge_kernel,
        out_shape=jax.ShapeDtypeStruct((ROW, width, tokens), jnp.bfloat16),
        in_specs=[vmem()],
        out_specs=vmem(),
        compiler_params=kernel_params(),
        name="merge",
    )(part)
    attention = lax.all_to_all(merged, "head", 0, 0)
    low = (own & 2) == 0
    other = lax.ppermute(quarter, "seq", [(g, g ^ 2) for g in range(count)])
    halves = jnp.stack((jnp.where(low, quarter, other), jnp.where(low, other, quarter)), axis=1)
    theirs = lax.ppermute(halves, "seq", [(g, g ^ 1) for g in range(count)])
    even = (own & 1) == 0
    w_mine = jnp.stack((jnp.where(even, halves, theirs), jnp.where(even, theirs, halves)), axis=2)
    mixed = lax.dot_general(
        attention.reshape(heads * width, tokens),
        w_mine.reshape(heads * width, columns),
        (((0,), (0,)), ((), ())),
        preferred_element_type=jnp.float32,
    )
    return mixed.astype(jnp.bfloat16)


def solution(mesh):
    return jax.shard_map(
        shards,
        mesh=mesh,
        in_specs=(
            P("seq", "head"),
            P("seq", "head"),
            P("seq", "head"),
            P("seq", "head"),
            P("seq", "head"),
            P(),
            P(),
            P(),
            P(),
            P("head", None),
        ),
        out_specs=P("seq", "head"),
        check_vma=False,
    )
```

```python
import functools

import jax
import jax.numpy as jnp
from jax import lax
from jax.experimental import pallas as pl
from jax.experimental.pallas import tpu as pltpu
from jax.sharding import PartitionSpec as P

HD = 128
BLK = 128
NEAR = 2
ROW = 8
TPAD = 16
NEG = -1e30
FLOOR = -1e9
SCORE_SCALE = HD ** (-0.5) * 1.4426950408889634
EARLY = (0, -1, 1, -2, 2)
LATE = (-3, 3, 4)
TOGETHER = 4
TEXT_ROWS = 8
GROUPS_AT_ONCE = 4
MESSAGE = 4 * BLK + TPAD
NEAR_AT = ROW
COUNT_AT = 32
WIDTH_AT = 40
LEN_AT = ROW + 1
WHERE_AT = ROW + 2


def row_peers():
    return [[z * ROW + r for r in range(ROW)] for z in range(ROW)]


def along_column(block, distance):
    count = ROW * ROW
    return lax.ppermute(block, "seq", [(g, (g + ROW * distance) % count) for g in range(count)])


def turned(buf):
    for a in range(2):
        for h in range(2):
            tile = buf[a * BLK : (a + 1) * BLK, h * HD : (h + 1) * HD].astype(jnp.float32)
            yield a, h, tile.T.astype(jnp.bfloat16)


def key_kernel(k_in, v_in, tk_in, tv_in, kv_out, v_buf, sems):
    copies = [
        pltpu.make_async_copy(v_in, v_buf, sems.at[0]),
        pltpu.make_async_copy(k_in, kv_out.at[: 2 * BLK], sems.at[1]),
    ]
    for copy in copies:
        copy.start()
    blank = jnp.zeros((TPAD - 2 * tk_in.shape[0], kv_out.shape[1]), jnp.float32)
    text = (tk_in[...].astype(jnp.float32), tv_in[...].astype(jnp.float32), blank)
    kv_out[4 * BLK :, :] = jnp.concatenate(text, axis=0).astype(jnp.bfloat16)
    copies[0].wait()
    for a, h, tile in turned(v_buf):
        kv_out[(2 + a) * BLK : (3 + a) * BLK, h * HD : (h + 1) * HD] = tile
    copies[1].wait()


def query_kernel(q_in, q_out, q_buf, sems):
    copy = pltpu.make_async_copy(q_in, q_buf, sems.at[0])
    copy.start()
    copy.wait()
    for a, h, tile in turned(q_buf):
        for i in range(ROW):
            q_out[i, a * BLK : (a + 1) * BLK, h * HD : (h + 1) * HD] = tile


def list_kernel(where_ref, far_ref, count_ref, width_ref, w_in, table_ref, w_out, wide, tall, sems):
    z = where_ref[0]
    r = where_ref[1]
    heads, quarter, columns = w_out.shape
    start = pl.multiple_of(((z & 1) * 2 + (r & 1)) * quarter, quarter)
    copies = [
        pltpu.make_async_copy(
            w_in.at[pl.ds(start, quarter), i * columns : (i + 1) * columns], w_out.at[i], sems.at[i]
        )
        for i in range(heads)
    ]
    for copy in copies:
        copy.start()
    rows = 2 * ROW
    slots = far_ref.shape[0]
    wide[...] = jnp.zeros(wide.shape, jnp.int32)
    wide[:slots, :] = far_ref[...]
    wide[COUNT_AT : COUNT_AT + 1, :] = count_ref[...]
    wide[WIDTH_AT : WIDTH_AT + 2 * NEAR + 1, : ROW * ROW] = width_ref[...]
    tall[...] = wide[...].T
    mine = tall[pl.ds(pl.multiple_of(z * rows, rows), rows), :]
    place = lax.broadcasted_iota(jnp.int32, mine.shape, 1)
    count = jnp.sum(jnp.where(place == COUNT_AT, mine, 0), axis=1, keepdims=True)
    live = (place < count) & (place < slots)
    lane = lax.broadcasted_iota(jnp.int32, (rows, BLK), 1)
    table = jnp.where(lane == LEN_AT, where_ref[2], 0)
    table = jnp.where(lane == WHERE_AT, z, table)
    table = jnp.where(lane == WHERE_AT + 1, r, table)
    for s, step in enumerate(EARLY + LATE):
        group = ((z + step) & (ROW - 1)) * ROW + r
        asked = jnp.where(live & ((mine >> 1) == group), 1 + (mine & 1), 0)
        table = jnp.where(lane == s, jnp.sum(asked, axis=1, keepdims=True), table)
    widths = tall[pl.ds(pl.multiple_of(z * ROW, ROW), ROW), :]
    place = lax.broadcasted_iota(jnp.int32, widths.shape, 1) - WIDTH_AT
    query = lax.broadcasted_iota(jnp.int32, widths.shape, 0)
    offset = (r - query + NEAR) & (ROW - 1)
    group = z * ROW + query + offset - NEAR
    valid = (group >= 0) & (group < ROW * ROW) & (place == offset)
    step = (group >> 3) - z
    slot = jnp.where(step == 0, 0, jnp.where(step < 0, 1, 2))
    near = jnp.sum(jnp.where(valid, widths * 16 + slot, 0), axis=1, keepdims=True)
    near = jnp.concatenate((near, jnp.zeros((rows - ROW, 1), jnp.int32)), axis=0)
    table_ref[...] = jnp.where(lane == NEAR_AT, near, table)
    for copy in copies:
        copy.wait()


def three_parts(x):
    high = x.astype(jnp.bfloat16).astype(jnp.float32)
    rest = x - high
    middle = rest.astype(jnp.bfloat16).astype(jnp.float32)
    return [high, middle, rest - middle]


def two_parts(x):
    high = x.astype(jnp.bfloat16).astype(jnp.float32)
    return [high, x - high]


def list_units(table, first, count, units):
    def one_block(i, n):
        for s in range(count):
            asked = table[i, first + s]
            units[n] = i * 16 + s * 2 + asked - 1
            n = n + jnp.where(asked > 0, 1, 0)
        return n

    return lax.fori_loop(0, 2 * ROW, one_block, jnp.int32(0))


def set_text(tiles, table, bias, text_k, text_v):
    z = table[0, WHERE_AT]
    r = table[0, WHERE_AT + 1]
    row = lax.broadcasted_iota(jnp.int32, (TEXT_ROWS, 2 * BLK), 0)
    keys = []
    vals = []
    for s, step in enumerate(EARLY + LATE):
        first = (((z + step) & (ROW - 1)) * ROW + r) * 4
        alive = (row < 4) & (first + row < table[0, LEN_AT])
        bias[s * TEXT_ROWS : (s + 1) * TEXT_ROWS, :] = jnp.where(alive, 0.0, NEG)
        tile = tiles[s].astype(jnp.float32)[:TEXT_ROWS]
        keys.append(tile)
        vals.append(pltpu.roll(tile, 4, 0))
    text_k[...] = jnp.concatenate(keys, axis=0).astype(jnp.bfloat16)
    vals.append(jnp.zeros((HD - ROW * TEXT_ROWS, 2 * HD), jnp.float32))
    vals = jnp.concatenate(vals, axis=0)
    for h in range(2):
        text_v[h] = vals[:, h * HD : (h + 1) * HD].T.astype(jnp.bfloat16)


def group_queries(q_ref, g, h):
    lanes = slice(h * HD, (h + 1) * HD)
    return jnp.concatenate((q_ref[g, :BLK, lanes], q_ref[g, BLK:, lanes]), axis=1)


def product(left, right):
    return jnp.dot(left, right, preferred_element_type=jnp.float32)


def head_rows(h):
    return slice(h * HD, (h + 1) * HD)


def text_step(q_ref, cases, text_k, text_v, bias):
    spare = HD - text_k.shape[0]
    scores = [
        product(text_k[:, head_rows(h)], group_queries(q_ref, g, h)) * SCORE_SCALE + bias[...] for g, h in cases
    ]
    tops = [jnp.maximum(jnp.max(s, axis=0, keepdims=True), FLOOR) for s in scores]
    weights = [jnp.exp2(s - top) for s, top in zip(scores, tops)]
    totals = [jnp.sum(p, axis=0, keepdims=True) for p in weights]
    filler = jnp.zeros((spare, 2 * BLK), jnp.bfloat16)
    outs = [
        product(text_v[h], jnp.concatenate((p.astype(jnp.bfloat16), filler), axis=0))
        for (_, h), p in zip(cases, weights)
    ]
    return list(zip(tops, totals, outs))


def group_cases(step, groups):
    return [(step * groups + j, h) for j in range(groups) for h in range(2)]


def joined(old, new):
    top = jnp.maximum(old[0], new[0])
    fade = jnp.exp2(old[0] - top)
    rise = jnp.exp2(new[0] - top)
    return top, old[1] * fade + new[1] * rise, old[2] * fade + new[2] * rise


def read_state(acc, stat, g, h):
    return stat[g, 2 * h : 2 * h + 1, :], stat[g, 2 * h + 1 : 2 * h + 2, :], acc[g, head_rows(h), :]


def write_state(acc, stat, g, h, state):
    stat[g, 2 * h : 2 * h + 1, :] = state[0]
    stat[g, 2 * h + 1 : 2 * h + 2, :] = state[1]
    acc[g, head_rows(h), :] = state[2]


def walk_units(units, count, q_ref, kv, acc, stat):
    def step(t, _):
        work = []
        for j in range(TOGETHER):
            number = t * TOGETHER + j
            code = jnp.where(number < count, units[number], 0)
            gone = jnp.where(number < count, 0.0, NEG)
            block = code >> 4
            g = block >> 1
            across = pl.multiple_of((block & 1) * BLK, BLK)
            who = (code & 15) >> 1
            down = pl.multiple_of((code & 1) * BLK, BLK)
            for h in range(2):
                s = product(
                    kv[who, pl.ds(down, BLK), head_rows(h)], q_ref[g, pl.ds(across, BLK), head_rows(h)]
                )
                work.append((g, across, who, down, h, gone, s * SCORE_SCALE))
        done = []
        for g, across, who, down, h, gone, s in work:
            top = jnp.max(s, axis=0, keepdims=True)
            p = jnp.exp2(s - top)
            total = jnp.sum(p, axis=0, keepdims=True)
            out = product(kv[who, pl.ds(down + 2 * BLK, BLK), head_rows(h)], p.astype(jnp.bfloat16))
            done.append((g, across, h, top + gone, total, out))
        for g, across, h, top, total, out in done:
            lanes = pl.ds(across, BLK)
            old_top = stat[g, 2 * h : 2 * h + 1, lanes]
            new_top = jnp.maximum(old_top, top)
            fade = jnp.exp2(old_top - new_top)
            rise = jnp.exp2(top - new_top)
            stat[g, 2 * h : 2 * h + 1, lanes] = new_top
            stat[g, 2 * h + 1 : 2 * h + 2, lanes] = (
                stat[g, 2 * h + 1 : 2 * h + 2, lanes] * fade + total * rise
            )
            acc[g, head_rows(h), lanes] = acc[g, head_rows(h), lanes] * fade + out * rise
        return 0

    lax.fori_loop(0, (count + TOGETHER - 1) // TOGETHER, step, 0)


def start_all(pairs, sems):
    copies = [pltpu.make_async_copy(src, dst, sems.at[i]) for i, (src, dst) in enumerate(pairs)]
    for copy in copies:
        copy.start()
    return [copy.wait for copy in copies]


def early_kernel(table, q_in, own, f1, b1, f2, b2, acc, stat, q_ref, kv, units, sems):
    waits = start_all([(x, kv.at[i]) for i, x in enumerate((own, f1, b1, f2, b2))] + [(q_in, q_ref)], sems)
    count = list_units(table, 0, len(EARLY), units)
    for wait in waits:
        wait()
    offset = lax.broadcasted_iota(jnp.int32, (2 * BLK, 2 * BLK), 0) - lax.broadcasted_iota(
        jnp.int32, (2 * BLK, 2 * BLK), 1
    )
    distance = jnp.abs(offset)

    def one_group(g, _):
        near = table[g, NEAR_AT]

        @pl.when(near > 0)
        def _():
            who = near & 15
            scores = []
            for h in range(2):
                s = product(kv[who, : 2 * BLK, head_rows(h)], group_queries(q_ref, g, h)) * SCORE_SCALE
                scores.append(jnp.where(distance < (near >> 4), s, NEG))
            fresh = []
            for h, s in enumerate(scores):
                top = jnp.maximum(jnp.max(s, axis=0, keepdims=True), FLOOR)
                p = jnp.exp2(s - top)
                values = jnp.concatenate(
                    (kv[who, 2 * BLK : 3 * BLK, head_rows(h)], kv[who, 3 * BLK : 4 * BLK, head_rows(h)]),
                    axis=1,
                )
                fresh.append((top, jnp.sum(p, axis=0, keepdims=True), product(values, p.astype(jnp.bfloat16))))
            for h, new in enumerate(fresh):
                write_state(acc, stat, g, h, new)
            stat[g, 4:8, :] = jnp.zeros((4, 2 * BLK), jnp.float32)

        @pl.when(near == 0)
        def _():
            acc[g, :, :] = jnp.zeros((2 * HD, 2 * BLK), jnp.float32)
            row = lax.broadcasted_iota(jnp.int32, (8, 2 * BLK), 0)
            stat[g, :, :] = jnp.where((row == 0) | (row == 2), FLOOR, 0.0)

        return 0

    lax.fori_loop(0, ROW, one_group, 0)
    walk_units(units, count, q_ref, kv, acc, stat)


def late_kernel(
    table, q_in, own, f1, b1, f2, b2, f3, b3, far4, acc_in, stat_in, out_ref, acc, stat,
    q_ref, kv, units, sems, tiles, bias, text_k, text_v,
):
    pairs = [(f3, kv.at[0]), (b3, kv.at[1]), (far4, kv.at[2]), (q_in, q_ref)]
    for i, x in enumerate((own, f1, b1, f2, b2, f3, b3, far4)):
        pairs.append((x.at[4 * BLK :], tiles.at[i]))
    waits = start_all(pairs, sems)
    count = list_units(table, len(EARLY), len(LATE), units)
    for wait in waits:
        wait()
    set_text(tiles, table, bias, text_k, text_v)
    walk_units(units, count, q_ref, kv, acc, stat)

    def some_groups(step, _):
        cases = group_cases(step, GROUPS_AT_ONCE)
        fresh = text_step(q_ref, cases, text_k, text_v, bias)
        done = [joined(read_state(acc, stat, g, h), new) for (g, h), new in zip(cases, fresh)]
        for x in range(0, len(cases), 2):
            g = cases[x][0]
            rows = []
            for h in range(2):
                top, total, out = done[x + h]
                out_ref[g, head_rows(h), :] = out.astype(jnp.bfloat16)
                rows += three_parts(top) + two_parts(total)
            rows.append(jnp.zeros((TPAD - len(rows), 2 * BLK), jnp.float32))
            out_ref[g, 2 * HD : 2 * HD + TPAD, :] = jnp.concatenate(rows, axis=0).astype(jnp.bfloat16)
        return 0

    lax.fori_loop(0, ROW // GROUPS_AT_ONCE, some_groups, 0)


def merge_kernel(part_ref, out_ref):
    stats = [part_ref[i, 2 * HD : 2 * HD + TPAD, :].astype(jnp.float32) for i in range(ROW)]
    for h in range(2):
        tops = [s[5 * h : 5 * h + 1] + s[5 * h + 1 : 5 * h + 2] + s[5 * h + 2 : 5 * h + 3] for s in stats]
        sums = [s[5 * h + 3 : 5 * h + 4] + s[5 * h + 4 : 5 * h + 5] for s in stats]
        top = functools.reduce(jnp.maximum, tops)
        weights = [jnp.exp2(t - top) for t in tops]
        total = functools.reduce(jnp.add, [w * s for w, s in zip(weights, sums)])
        inverse = 1.0 / total
        rows = slice(h * HD, (h + 1) * HD)
        acc = None
        for i in range(ROW):
            term = part_ref[i, rows, :].astype(jnp.float32) * weights[i]
            acc = term if acc is None else acc + term
        acc = (acc * inverse).astype(jnp.bfloat16)
        for i in range(ROW):
            out_ref[i, rows, :] = acc


def smem():
    return pl.BlockSpec(memory_space=pltpu.SMEM)


def vmem():
    return pl.BlockSpec(memory_space=pltpu.VMEM)


def anywhere():
    return pl.BlockSpec(memory_space=pl.ANY)


def kernel_params():
    return pltpu.CompilerParams(vmem_limit_bytes=32 << 20)


def attend_scratch(slots, copies):
    return [
        pltpu.VMEM((ROW, 2 * BLK, 2 * HD), jnp.bfloat16),
        pltpu.VMEM((slots, MESSAGE, 2 * HD), jnp.bfloat16),
        pltpu.SMEM((2 * ROW * slots + 8,), jnp.int32),
        pltpu.SemaphoreType.DMA((copies,)),
    ]


def text_scratch():
    return [
        pltpu.VMEM((ROW, TPAD, 2 * HD), jnp.bfloat16),
        pltpu.VMEM((ROW * TEXT_ROWS, 2 * BLK), jnp.float32),
        pltpu.VMEM((ROW * TEXT_ROWS, 2 * HD), jnp.bfloat16),
        pltpu.VMEM((2, HD, HD), jnp.bfloat16),
    ]


def shards(
    queries,
    keys,
    values,
    text_keys,
    text_values,
    text_len,
    radial_width,
    far_blocks,
    far_count,
    w_out,
):
    own = lax.axis_index("seq")
    where = jnp.stack((own // ROW, own % ROW, text_len[0])).astype(jnp.int32)
    tokens, width = queries.shape
    heads = lax.axis_size("head")
    columns = w_out.shape[1] // heads

    whole = pltpu.CompilerParams(vmem_limit_bytes=60 << 20)
    kv = pl.pallas_call(
        key_kernel,
        out_shape=jax.ShapeDtypeStruct((MESSAGE, width), jnp.bfloat16),
        in_specs=[anywhere(), anywhere(), vmem(), vmem()],
        out_specs=vmem(),
        scratch_shapes=[pltpu.VMEM((tokens, width), jnp.bfloat16), pltpu.SemaphoreType.DMA((2,))],
        compiler_params=whole,
        name="key_message",
    )(keys, values, text_keys, text_values)
    kv, queries = lax.optimization_barrier((kv, queries))
    q_mine = pl.pallas_call(
        query_kernel,
        out_shape=jax.ShapeDtypeStruct((ROW, tokens, width), jnp.bfloat16),
        in_specs=[anywhere()],
        out_specs=vmem(),
        scratch_shapes=[pltpu.VMEM((tokens, width), jnp.bfloat16), pltpu.SemaphoreType.DMA((1,))],
        compiler_params=whole,
        name="query_message",
    )(queries)
    table, quarter = pl.pallas_call(
        list_kernel,
        out_shape=(
            jax.ShapeDtypeStruct((2 * ROW, BLK), jnp.int32),
            jax.ShapeDtypeStruct((heads, width // 4, columns), jnp.bfloat16),
        ),
        in_specs=[smem(), vmem(), vmem(), vmem(), anywhere()],
        out_specs=(vmem(), vmem()),
        scratch_shapes=[
            pltpu.VMEM((BLK, BLK), jnp.int32),
            pltpu.VMEM((BLK, BLK), jnp.int32),
            pltpu.SemaphoreType.DMA((heads,)),
        ],
        compiler_params=whole,
        cost_estimate=pl.CostEstimate(flops=40 * 10**9, bytes_accessed=10**5, transcendentals=0),
        name="lists",
    )(where, far_blocks.T, far_count[None, :], radial_width.T, w_out)

    count = ROW * ROW
    f1 = along_column(kv, 1)
    b1 = along_column(kv, -1)
    q_all = lax.all_to_all(q_mine, "seq", 0, 0, axis_index_groups=row_peers())
    f2 = along_column(kv, 2)
    b2 = along_column(kv, -2)
    f2, b2, table, quarter = lax.optimization_barrier((f2, b2, table, quarter))
    f3 = along_column(f2, 1)
    b3 = along_column(b2, -1)
    far4 = lax.ppermute(
        jnp.where(own % 2 == 0, f2, b2),
        "seq",
        [(g, (g + (2 * ROW if g % 2 == 0 else -2 * ROW)) % count) for g in range(count)],
    )
    quarter, q_all = lax.optimization_barrier((quarter, q_all))
    quarter = lax.all_to_all(quarter, "head", 0, 0)

    acc, stat = pl.pallas_call(
        early_kernel,
        out_shape=(
            jax.ShapeDtypeStruct((ROW, width, tokens), jnp.float32),
            jax.ShapeDtypeStruct((ROW, 8, tokens), jnp.float32),
        ),
        in_specs=[smem()] + [anywhere()] * 6,
        out_specs=(vmem(), vmem()),
        scratch_shapes=attend_scratch(len(EARLY), 6),
        compiler_params=kernel_params(),
        cost_estimate=pl.CostEstimate(flops=6 * 10**9, bytes_accessed=5 * 10**6, transcendentals=0),
        name="attend_early",
    )(table, q_all, kv, f1, b1, f2, b2)
    part, _, _ = pl.pallas_call(
        late_kernel,
        out_shape=(
            jax.ShapeDtypeStruct((ROW, width + TPAD, tokens), jnp.bfloat16),
            jax.ShapeDtypeStruct(acc.shape, acc.dtype),
            jax.ShapeDtypeStruct(stat.shape, stat.dtype),
        ),
        in_specs=[smem()] + [anywhere()] * 9 + [vmem()] * 2,
        out_specs=(vmem(),) * 3,
        scratch_shapes=attend_scratch(len(LATE), 4 + ROW) + text_scratch(),
        input_output_aliases={10: 1, 11: 2},
        compiler_params=kernel_params(),
        cost_estimate=pl.CostEstimate(flops=4 * 10**9, bytes_accessed=5 * 10**6, transcendentals=0),
        name="attend_late",
    )(table, q_all, kv, f1, b1, f2, b2, f3, b3, far4, acc, stat)
    part, quarter = lax.optimization_barrier((part, quarter))
    part = lax.all_to_all(part, "seq", 0, 0, axis_index_groups=row_peers())
    low = (own & ROW) == 0
    other = lax.ppermute(quarter, "seq", [(g, g ^ ROW) for g in range(count)])
    halves = jnp.stack((jnp.where(low, quarter, other), jnp.where(low, other, quarter)), axis=1)
    theirs = lax.ppermute(halves, "seq", [(g, g ^ 1) for g in range(count)])
    even = (own & 1) == 0
    w_mine = jnp.stack((jnp.where(even, halves, theirs), jnp.where(even, theirs, halves)), axis=2)
    merged = pl.pallas_call(
        merge_kernel,
        out_shape=jax.ShapeDtypeStruct((ROW, width, tokens), jnp.bfloat16),
        in_specs=[vmem()],
        out_specs=vmem(),
        compiler_params=kernel_params(),
        name="merge",
    )(part)
    attention = lax.all_to_all(merged, "head", 0, 0)
    mixed = lax.dot_general(
        attention.reshape(heads * width, tokens),
        w_mine.reshape(heads * width, columns),
        (((0,), (0,)), ((), ())),
        preferred_element_type=jnp.float32,
    )
    return mixed.astype(jnp.bfloat16)


def solution(mesh):
    return jax.shard_map(
        shards,
        mesh=mesh,
        in_specs=(
            P("seq", "head"),
            P("seq", "head"),
            P("seq", "head"),
            P("seq", "head"),
            P("seq", "head"),
            P(),
            P(),
            P(),
            P(),
            P("head", None),
        ),
        out_specs=P("seq", "head"),
        check_vma=False,
    )
```

```python
import functools

import jax
import jax.numpy as jnp
from jax import lax
from jax.experimental import pallas as pl
from jax.experimental.pallas import tpu as pltpu
from jax.sharding import PartitionSpec as P

HD = 128
BLK = 128
NEAR = 2
ROW = 8
TPAD = 16
NEG = -1e30
FLOOR = -1e9
SCORE_SCALE = HD ** (-0.5) * 1.4426950408889634
EARLY = (0, -1, 1, -2, 2)
LATE = (-3, 3, 4)
TOGETHER = 8
TEXT_ROWS = 8
GROUPS_AT_ONCE = 8
MESSAGE = 4 * BLK + TPAD
NEAR_AT = ROW
COUNT_AT = 32
WIDTH_AT = 40
LEN_AT = ROW + 1
WHERE_AT = ROW + 2


def row_peers():
    return [[z * ROW + r for r in range(ROW)] for z in range(ROW)]


def along_column(block, distance):
    count = ROW * ROW
    return lax.ppermute(block, "seq", [(g, (g + ROW * distance) % count) for g in range(count)])


def turned(buf):
    for a in range(2):
        for h in range(2):
            tile = buf[a * BLK : (a + 1) * BLK, h * HD : (h + 1) * HD].astype(jnp.float32)
            yield a, h, tile.T.astype(jnp.bfloat16)


def message_kernel(k_in, v_in, q_in, tk_in, tv_in, kv_out, q_out, v_buf, q_buf, sems):
    copies = [
        pltpu.make_async_copy(v_in, v_buf, sems.at[0]),
        pltpu.make_async_copy(q_in, q_buf, sems.at[1]),
        pltpu.make_async_copy(k_in, kv_out.at[: 2 * BLK], sems.at[2]),
    ]
    for copy in copies:
        copy.start()
    blank = jnp.zeros((TPAD - 2 * tk_in.shape[0], kv_out.shape[1]), jnp.float32)
    text = (tk_in[...].astype(jnp.float32), tv_in[...].astype(jnp.float32), blank)
    kv_out[4 * BLK :, :] = jnp.concatenate(text, axis=0).astype(jnp.bfloat16)
    copies[0].wait()
    for a, h, tile in turned(v_buf):
        kv_out[(2 + a) * BLK : (3 + a) * BLK, h * HD : (h + 1) * HD] = tile
    copies[1].wait()
    for a, h, tile in turned(q_buf):
        for i in range(ROW):
            q_out[i, a * BLK : (a + 1) * BLK, h * HD : (h + 1) * HD] = tile
    copies[2].wait()


def list_kernel(where_ref, far_ref, count_ref, width_ref, w_in, table_ref, w_out, wide, tall, sems):
    z = where_ref[0]
    r = where_ref[1]
    heads, quarter, columns = w_out.shape
    start = pl.multiple_of(((z & 1) * 2 + (r & 1)) * quarter, quarter)
    copies = [
        pltpu.make_async_copy(
            w_in.at[pl.ds(start, quarter), i * columns : (i + 1) * columns], w_out.at[i], sems.at[i]
        )
        for i in range(heads)
    ]
    for copy in copies:
        copy.start()
    rows = 2 * ROW
    slots = far_ref.shape[0]
    wide[...] = jnp.zeros(wide.shape, jnp.int32)
    wide[:slots, :] = far_ref[...]
    wide[COUNT_AT : COUNT_AT + 1, :] = count_ref[...]
    wide[WIDTH_AT : WIDTH_AT + 2 * NEAR + 1, : ROW * ROW] = width_ref[...]
    tall[...] = wide[...].T
    mine = tall[pl.ds(pl.multiple_of(z * rows, rows), rows), :]
    place = lax.broadcasted_iota(jnp.int32, mine.shape, 1)
    count = jnp.sum(jnp.where(place == COUNT_AT, mine, 0), axis=1, keepdims=True)
    live = (place < count) & (place < slots)
    lane = lax.broadcasted_iota(jnp.int32, (rows, BLK), 1)
    table = jnp.where(lane == LEN_AT, where_ref[2], 0)
    table = jnp.where(lane == WHERE_AT, z, table)
    table = jnp.where(lane == WHERE_AT + 1, r, table)
    for s, step in enumerate(EARLY + LATE):
        group = ((z + step) & (ROW - 1)) * ROW + r
        asked = jnp.where(live & ((mine >> 1) == group), 1 + (mine & 1), 0)
        table = jnp.where(lane == s, jnp.sum(asked, axis=1, keepdims=True), table)
    widths = tall[pl.ds(pl.multiple_of(z * ROW, ROW), ROW), :]
    place = lax.broadcasted_iota(jnp.int32, widths.shape, 1) - WIDTH_AT
    query = lax.broadcasted_iota(jnp.int32, widths.shape, 0)
    offset = (r - query + NEAR) & (ROW - 1)
    group = z * ROW + query + offset - NEAR
    valid = (group >= 0) & (group < ROW * ROW) & (place == offset)
    step = (group >> 3) - z
    slot = jnp.where(step == 0, 0, jnp.where(step < 0, 1, 2))
    near = jnp.sum(jnp.where(valid, widths * 16 + slot, 0), axis=1, keepdims=True)
    near = jnp.concatenate((near, jnp.zeros((rows - ROW, 1), jnp.int32)), axis=0)
    table_ref[...] = jnp.where(lane == NEAR_AT, near, table)
    for copy in copies:
        copy.wait()


def three_parts(x):
    high = x.astype(jnp.bfloat16).astype(jnp.float32)
    rest = x - high
    middle = rest.astype(jnp.bfloat16).astype(jnp.float32)
    return [high, middle, rest - middle]


def two_parts(x):
    high = x.astype(jnp.bfloat16).astype(jnp.float32)
    return [high, x - high]


def list_units(table, first, count, units):
    def one_block(i, n):
        for s in range(count):
            asked = table[i, first + s]
            units[n] = i * 16 + s * 2 + asked - 1
            n = n + jnp.where(asked > 0, 1, 0)
        return n

    return lax.fori_loop(0, 2 * ROW, one_block, jnp.int32(0))


def set_text(tiles, table, bias, text_k, text_v):
    z = table[0, WHERE_AT]
    r = table[0, WHERE_AT + 1]
    row = lax.broadcasted_iota(jnp.int32, (TEXT_ROWS, 2 * BLK), 0)
    keys = []
    vals = []
    for s, step in enumerate(EARLY + LATE):
        first = (((z + step) & (ROW - 1)) * ROW + r) * 4
        alive = (row < 4) & (first + row < table[0, LEN_AT])
        bias[s * TEXT_ROWS : (s + 1) * TEXT_ROWS, :] = jnp.where(alive, 0.0, NEG)
        tile = tiles[s].astype(jnp.float32)[:TEXT_ROWS]
        keys.append(tile)
        vals.append(pltpu.roll(tile, 4, 0))
    text_k[...] = jnp.concatenate(keys, axis=0).astype(jnp.bfloat16)
    spare = HD - ROW * TEXT_ROWS
    vals.append(jnp.zeros((spare, 2 * HD), jnp.float32))
    vals = jnp.concatenate(vals, axis=0)
    for h in range(2):
        text_v[h] = vals[:, h * HD : (h + 1) * HD].T.astype(jnp.bfloat16)[:, : HD - spare]


def group_queries(q_ref, g, h):
    lanes = slice(h * HD, (h + 1) * HD)
    return jnp.concatenate((q_ref[g, :BLK, lanes], q_ref[g, BLK:, lanes]), axis=1)


def product(left, right):
    return jnp.dot(left, right, preferred_element_type=jnp.float32)


def head_rows(h):
    return slice(h * HD, (h + 1) * HD)


def text_step(q_ref, cases, text_k, text_v, bias):
    scores = [
        product(text_k[:, head_rows(h)], group_queries(q_ref, g, h)) * SCORE_SCALE + bias[...] for g, h in cases
    ]
    tops = [jnp.maximum(jnp.max(s, axis=0, keepdims=True), FLOOR) for s in scores]
    weights = [jnp.exp2(s - top) for s, top in zip(scores, tops)]
    totals = [jnp.sum(p, axis=0, keepdims=True) for p in weights]
    outs = [product(text_v[h], p.astype(jnp.bfloat16)) for (_, h), p in zip(cases, weights)]
    return list(zip(tops, totals, outs))


def group_cases(step, groups):
    return [(step * groups + j, h) for j in range(groups) for h in range(2)]


def joined(old, new):
    top = jnp.maximum(old[0], new[0])
    fade = jnp.exp2(old[0] - top)
    rise = jnp.exp2(new[0] - top)
    return top, old[1] * fade + new[1] * rise, old[2] * fade + new[2] * rise


def read_state(acc, stat, g, h):
    return stat[g, 2 * h : 2 * h + 1, :], stat[g, 2 * h + 1 : 2 * h + 2, :], acc[g, head_rows(h), :]


def write_state(acc, stat, g, h, state):
    stat[g, 2 * h : 2 * h + 1, :] = state[0]
    stat[g, 2 * h + 1 : 2 * h + 2, :] = state[1]
    acc[g, head_rows(h), :] = state[2]


def walk_units(units, count, q_ref, kv, acc, stat):
    def step(t, _):
        work = []
        for j in range(TOGETHER):
            number = t * TOGETHER + j
            code = jnp.where(number < count, units[number], 0)
            gone = jnp.where(number < count, 0.0, NEG)
            block = code >> 4
            g = block >> 1
            across = pl.multiple_of((block & 1) * BLK, BLK)
            who = (code & 15) >> 1
            down = pl.multiple_of((code & 1) * BLK, BLK)
            for h in range(2):
                s = product(
                    kv[who, pl.ds(down, BLK), head_rows(h)], q_ref[g, pl.ds(across, BLK), head_rows(h)]
                )
                work.append((g, across, who, down, h, gone, s * SCORE_SCALE))
        done = []
        for g, across, who, down, h, gone, s in work:
            top = jnp.max(s, axis=0, keepdims=True)
            p = jnp.exp2(s - top)
            total = jnp.sum(p, axis=0, keepdims=True)
            out = product(kv[who, pl.ds(down + 2 * BLK, BLK), head_rows(h)], p.astype(jnp.bfloat16))
            done.append((g, across, h, top + gone, total, out))
        for g, across, h, top, total, out in done:
            lanes = pl.ds(across, BLK)
            old_top = stat[g, 2 * h : 2 * h + 1, lanes]
            new_top = jnp.maximum(old_top, top)
            fade = jnp.exp2(old_top - new_top)
            rise = jnp.exp2(top - new_top)
            stat[g, 2 * h : 2 * h + 1, lanes] = new_top
            stat[g, 2 * h + 1 : 2 * h + 2, lanes] = (
                stat[g, 2 * h + 1 : 2 * h + 2, lanes] * fade + total * rise
            )
            acc[g, head_rows(h), lanes] = acc[g, head_rows(h), lanes] * fade + out * rise
        return 0

    lax.fori_loop(0, (count + TOGETHER - 1) // TOGETHER, step, 0)


def start_all(pairs, sems):
    copies = [pltpu.make_async_copy(src, dst, sems.at[i]) for i, (src, dst) in enumerate(pairs)]
    for copy in copies:
        copy.start()
    return [copy.wait for copy in copies]


def early_kernel(table, q_ref, own, f1, b1, f2, b2, acc, stat, kv, units, sems):
    waits = start_all([(x, kv.at[i]) for i, x in enumerate((own, f1, b1, f2, b2))], sems)
    count = list_units(table, 0, len(EARLY), units)
    for wait in waits:
        wait()
    offset = lax.broadcasted_iota(jnp.int32, (2 * BLK, 2 * BLK), 0) - lax.broadcasted_iota(
        jnp.int32, (2 * BLK, 2 * BLK), 1
    )
    distance = jnp.abs(offset)

    r = table[0, WHERE_AT + 1]
    for steps in ((0, 1), (2, 3), (4,)):
        cases = []
        for step in steps:
            g = (r + NEAR - step) & (ROW - 1)
            near = table[g, NEAR_AT]
            who = near & 15
            for h in range(2):
                s = product(kv[who, : 2 * BLK, head_rows(h)], group_queries(q_ref, g, h)) * SCORE_SCALE
                cases.append((g, h, who, jnp.where(distance < (near >> 4), s, NEG)))
        fresh = []
        for g, h, who, s in cases:
            top = jnp.maximum(jnp.max(s, axis=0, keepdims=True), FLOOR)
            p = jnp.exp2(s - top)
            values = jnp.concatenate(
                (kv[who, 2 * BLK : 3 * BLK, head_rows(h)], kv[who, 3 * BLK : 4 * BLK, head_rows(h)]), axis=1
            )
            out = product(values, p.astype(jnp.bfloat16))
            fresh.append((g, h, (top, jnp.sum(p, axis=0, keepdims=True), out)))
        for g, h, state in fresh:
            write_state(acc, stat, g, h, state)
            stat[g, 4:8, :] = jnp.zeros((4, 2 * BLK), jnp.float32)
    row = lax.broadcasted_iota(jnp.int32, (8, 2 * BLK), 0)
    for step in range(2 * NEAR + 1, ROW):
        g = (r + NEAR - step) & (ROW - 1)
        acc[g, :, :] = jnp.zeros((2 * HD, 2 * BLK), jnp.float32)
        stat[g, :, :] = jnp.where((row == 0) | (row == 2), FLOOR, 0.0)
    walk_units(units, count, q_ref, kv, acc, stat)


def late_kernel(
    table, q_ref, own, f1, b1, f2, b2, f3, b3, far4, acc_in, stat_in, out_ref, acc, stat,
    kv, units, sems, tiles, bias, text_k, text_v,
):
    pairs = [(f3, kv.at[0]), (b3, kv.at[1]), (far4, kv.at[2])]
    for i, x in enumerate((own, f1, b1, f2, b2, f3, b3, far4)):
        pairs.append((x.at[4 * BLK :], tiles.at[i]))
    waits = start_all(pairs, sems)
    count = list_units(table, len(EARLY), len(LATE), units)
    for wait in waits:
        wait()
    set_text(tiles, table, bias, text_k, text_v)
    walk_units(units, count, q_ref, kv, acc, stat)

    def some_groups(step, _):
        cases = group_cases(step, GROUPS_AT_ONCE)
        fresh = text_step(q_ref, cases, text_k, text_v, bias)
        done = [joined(read_state(acc, stat, g, h), new) for (g, h), new in zip(cases, fresh)]
        for x in range(0, len(cases), 2):
            g = cases[x][0]
            rows = []
            for h in range(2):
                top, total, out = done[x + h]
                out_ref[g, head_rows(h), :] = out.astype(jnp.bfloat16)
                rows += three_parts(top) + two_parts(total)
            rows.append(jnp.zeros((TPAD - len(rows), 2 * BLK), jnp.float32))
            out_ref[g, 2 * HD : 2 * HD + TPAD, :] = jnp.concatenate(rows, axis=0).astype(jnp.bfloat16)
        return 0

    lax.fori_loop(0, ROW // GROUPS_AT_ONCE, some_groups, 0)


def merge_kernel(part_ref, out_ref):
    stats = [part_ref[i, 2 * HD : 2 * HD + TPAD, :].astype(jnp.float32) for i in range(ROW)]
    for h in range(2):
        tops = [s[5 * h : 5 * h + 1] + s[5 * h + 1 : 5 * h + 2] + s[5 * h + 2 : 5 * h + 3] for s in stats]
        sums = [s[5 * h + 3 : 5 * h + 4] + s[5 * h + 4 : 5 * h + 5] for s in stats]
        top = functools.reduce(jnp.maximum, tops)
        weights = [jnp.exp2(t - top) for t in tops]
        total = functools.reduce(jnp.add, [w * s for w, s in zip(weights, sums)])
        inverse = 1.0 / total
        rows = slice(h * HD, (h + 1) * HD)
        acc = None
        for i in range(ROW):
            term = part_ref[i, rows, :].astype(jnp.float32) * weights[i]
            acc = term if acc is None else acc + term
        acc = (acc * inverse).astype(jnp.bfloat16)
        for i in range(ROW):
            out_ref[i, rows, :] = acc


def smem():
    return pl.BlockSpec(memory_space=pltpu.SMEM)


def vmem():
    return pl.BlockSpec(memory_space=pltpu.VMEM)


def anywhere():
    return pl.BlockSpec(memory_space=pl.ANY)


def kernel_params():
    return pltpu.CompilerParams(vmem_limit_bytes=32 << 20)


def attend_scratch(slots, copies):
    return [
        pltpu.VMEM((slots, MESSAGE, 2 * HD), jnp.bfloat16),
        pltpu.SMEM((2 * ROW * slots + 8,), jnp.int32),
        pltpu.SemaphoreType.DMA((copies,)),
    ]


def text_scratch():
    return [
        pltpu.VMEM((ROW, TPAD, 2 * HD), jnp.bfloat16),
        pltpu.VMEM((ROW * TEXT_ROWS, 2 * BLK), jnp.float32),
        pltpu.VMEM((ROW * TEXT_ROWS, 2 * HD), jnp.bfloat16),
        pltpu.VMEM((2, HD, ROW * TEXT_ROWS), jnp.bfloat16),
    ]


def shards(
    queries,
    keys,
    values,
    text_keys,
    text_values,
    text_len,
    radial_width,
    far_blocks,
    far_count,
    w_out,
):
    own = lax.axis_index("seq")
    where = jnp.stack((own // ROW, own % ROW, text_len[0])).astype(jnp.int32)
    tokens, width = queries.shape
    heads = lax.axis_size("head")
    columns = w_out.shape[1] // heads

    whole = pltpu.CompilerParams(vmem_limit_bytes=60 << 20)
    kv, q_mine = pl.pallas_call(
        message_kernel,
        out_shape=(
            jax.ShapeDtypeStruct((MESSAGE, width), jnp.bfloat16),
            jax.ShapeDtypeStruct((ROW, tokens, width), jnp.bfloat16),
        ),
        in_specs=[anywhere()] * 3 + [vmem()] * 2,
        out_specs=(vmem(), vmem()),
        scratch_shapes=[
            pltpu.VMEM((tokens, width), jnp.bfloat16),
            pltpu.VMEM((tokens, width), jnp.bfloat16),
            pltpu.SemaphoreType.DMA((3,)),
        ],
        compiler_params=whole,
        name="messages",
    )(keys, values, queries, text_keys, text_values)
    table, quarter = pl.pallas_call(
        list_kernel,
        out_shape=(
            jax.ShapeDtypeStruct((2 * ROW, BLK), jnp.int32),
            jax.ShapeDtypeStruct((heads, width // 4, columns), jnp.bfloat16),
        ),
        in_specs=[smem(), vmem(), vmem(), vmem(), anywhere()],
        out_specs=(vmem(), vmem()),
        scratch_shapes=[
            pltpu.VMEM((BLK, BLK), jnp.int32),
            pltpu.VMEM((BLK, BLK), jnp.int32),
            pltpu.SemaphoreType.DMA((heads,)),
        ],
        compiler_params=whole,
        cost_estimate=pl.CostEstimate(flops=40 * 10**9, bytes_accessed=10**5, transcendentals=0),
        name="lists",
    )(where, far_blocks.T, far_count[None, :], radial_width.T, w_out)

    count = ROW * ROW
    f1 = along_column(kv, 1)
    b1 = along_column(kv, -1)
    q_all = lax.all_to_all(q_mine, "seq", 0, 0, axis_index_groups=row_peers())
    f2 = along_column(kv, 2)
    b2 = along_column(kv, -2)
    f2, b2, table, quarter = lax.optimization_barrier((f2, b2, table, quarter))
    f3 = along_column(f2, 1)
    b3 = along_column(b2, -1)
    far4 = lax.ppermute(
        jnp.where(own % 2 == 0, f2, b2),
        "seq",
        [(g, (g + (2 * ROW if g % 2 == 0 else -2 * ROW)) % count) for g in range(count)],
    )
    quarter, q_all = lax.optimization_barrier((quarter, q_all))
    quarter = lax.all_to_all(quarter, "head", 0, 0)

    acc, stat = pl.pallas_call(
        early_kernel,
        out_shape=(
            jax.ShapeDtypeStruct((ROW, width, tokens), jnp.float32),
            jax.ShapeDtypeStruct((ROW, 8, tokens), jnp.float32),
        ),
        in_specs=[smem(), vmem()] + [anywhere()] * 5,
        out_specs=(vmem(), vmem()),
        scratch_shapes=attend_scratch(len(EARLY), 5),
        compiler_params=kernel_params(),
        cost_estimate=pl.CostEstimate(flops=6 * 10**9, bytes_accessed=5 * 10**6, transcendentals=0),
        name="attend_early",
    )(table, q_all, kv, f1, b1, f2, b2)
    part, _, _ = pl.pallas_call(
        late_kernel,
        out_shape=(
            jax.ShapeDtypeStruct((ROW, width + TPAD, tokens), jnp.bfloat16),
            jax.ShapeDtypeStruct(acc.shape, acc.dtype),
            jax.ShapeDtypeStruct(stat.shape, stat.dtype),
        ),
        in_specs=[smem(), vmem()] + [anywhere()] * 8 + [vmem()] * 2,
        out_specs=(vmem(),) * 3,
        scratch_shapes=attend_scratch(len(LATE), 3 + ROW) + text_scratch(),
        input_output_aliases={10: 1, 11: 2},
        compiler_params=kernel_params(),
        cost_estimate=pl.CostEstimate(flops=4 * 10**9, bytes_accessed=5 * 10**6, transcendentals=0),
        name="attend_late",
    )(table, q_all, kv, f1, b1, f2, b2, f3, b3, far4, acc, stat)
    part, quarter = lax.optimization_barrier((part, quarter))
    part = lax.all_to_all(part, "seq", 0, 0, axis_index_groups=row_peers())
    low = (own & ROW) == 0
    other = lax.ppermute(quarter, "seq", [(g, g ^ ROW) for g in range(count)])
    halves = jnp.stack((jnp.where(low, quarter, other), jnp.where(low, other, quarter)), axis=1)
    theirs = lax.ppermute(halves, "seq", [(g, g ^ 1) for g in range(count)])
    even = (own & 1) == 0
    w_mine = jnp.stack((jnp.where(even, halves, theirs), jnp.where(even, theirs, halves)), axis=2)
    merged = pl.pallas_call(
        merge_kernel,
        out_shape=jax.ShapeDtypeStruct((ROW, width, tokens), jnp.bfloat16),
        in_specs=[vmem()],
        out_specs=vmem(),
        compiler_params=kernel_params(),
        name="merge",
    )(part)
    attention = lax.all_to_all(merged, "head", 0, 0)
    mixed = lax.dot_general(
        attention.reshape(heads * width, tokens),
        w_mine.reshape(heads * width, columns),
        (((0,), (0,)), ((), ())),
        preferred_element_type=jnp.float32,
    )
    return mixed.astype(jnp.bfloat16)


def solution(mesh):
    return jax.shard_map(
        shards,
        mesh=mesh,
        in_specs=(
            P("seq", "head"),
            P("seq", "head"),
            P("seq", "head"),
            P("seq", "head"),
            P("seq", "head"),
            P(),
            P(),
            P(),
            P(),
            P("head", None),
        ),
        out_specs=P("seq", "head"),
        check_vma=False,
    )
```

```python
import functools

import jax
import jax.numpy as jnp
from jax import lax
from jax.experimental import pallas as pl
from jax.experimental.pallas import tpu as pltpu
from jax.sharding import PartitionSpec as P

HD = 128
BLK = 128
NEAR = 2
ROW = 8
TPAD = 16
NEG = -1e30
FLOOR = -1e9
SCORE_SCALE = HD ** (-0.5) * 1.4426950408889634
EARLY = (0, -1, 1, -2, 2)
LATE = (-3, 3, 4)
TOGETHER = 8
TEXT_ROWS = 8
GROUPS_AT_ONCE = 8
MESSAGE = 4 * BLK + TPAD
NEAR_AT = ROW
COUNT_AT = 32
WIDTH_AT = 40
LEN_AT = ROW + 1
WHERE_AT = ROW + 2


def row_peers():
    return [[z * ROW + r for r in range(ROW)] for z in range(ROW)]


def along_column(block, distance):
    count = ROW * ROW
    return lax.ppermute(block, "seq", [(g, (g + ROW * distance) % count) for g in range(count)])


def turned(buf):
    for a in range(2):
        for h in range(2):
            tile = buf[a * BLK : (a + 1) * BLK, h * HD : (h + 1) * HD].astype(jnp.float32)
            yield a, h, tile.T.astype(jnp.bfloat16)


def message_kernel(k_in, v_in, q_in, tk_in, tv_in, kv_out, q_out, v_buf, q_buf, sems):
    copies = [
        pltpu.make_async_copy(v_in, v_buf, sems.at[0]),
        pltpu.make_async_copy(q_in, q_buf, sems.at[1]),
        pltpu.make_async_copy(k_in, kv_out.at[: 2 * BLK], sems.at[2]),
    ]
    for copy in copies:
        copy.start()
    blank = jnp.zeros((TPAD - 2 * tk_in.shape[0], kv_out.shape[1]), jnp.float32)
    text = (tk_in[...].astype(jnp.float32), tv_in[...].astype(jnp.float32), blank)
    kv_out[4 * BLK :, :] = jnp.concatenate(text, axis=0).astype(jnp.bfloat16)
    copies[0].wait()
    for a, h, tile in turned(v_buf):
        kv_out[(2 + a) * BLK : (3 + a) * BLK, h * HD : (h + 1) * HD] = tile
    copies[1].wait()
    for a, h, tile in turned(q_buf):
        for i in range(ROW):
            q_out[i, a * BLK : (a + 1) * BLK, h * HD : (h + 1) * HD] = tile
    copies[2].wait()


def list_kernel(where_ref, far_ref, count_ref, width_ref, w_in, table_ref, w_out, wide, tall, sems):
    z = where_ref[0]
    r = where_ref[1]
    heads, quarter, columns = w_out.shape
    start = pl.multiple_of(((z & 1) * 2 + (r & 1)) * quarter, quarter)
    copies = [
        pltpu.make_async_copy(
            w_in.at[pl.ds(start, quarter), i * columns : (i + 1) * columns], w_out.at[i], sems.at[i]
        )
        for i in range(heads)
    ]
    for copy in copies:
        copy.start()
    rows = 2 * ROW
    slots = far_ref.shape[0]
    wide[...] = jnp.zeros(wide.shape, jnp.int32)
    wide[:slots, :] = far_ref[...]
    wide[COUNT_AT : COUNT_AT + 1, :] = count_ref[...]
    wide[WIDTH_AT : WIDTH_AT + 2 * NEAR + 1, : ROW * ROW] = width_ref[...]
    tall[...] = wide[...].T
    mine = tall[pl.ds(pl.multiple_of(z * rows, rows), rows), :]
    place = lax.broadcasted_iota(jnp.int32, mine.shape, 1)
    count = jnp.sum(jnp.where(place == COUNT_AT, mine, 0), axis=1, keepdims=True)
    live = (place < count) & (place < slots)
    lane = lax.broadcasted_iota(jnp.int32, (rows, BLK), 1)
    table = jnp.where(lane == LEN_AT, where_ref[2], 0)
    table = jnp.where(lane == WHERE_AT, z, table)
    table = jnp.where(lane == WHERE_AT + 1, r, table)
    for s, step in enumerate(EARLY + LATE):
        group = ((z + step) & (ROW - 1)) * ROW + r
        asked = jnp.where(live & ((mine >> 1) == group), 1 + (mine & 1), 0)
        table = jnp.where(lane == s, jnp.sum(asked, axis=1, keepdims=True), table)
    widths = tall[pl.ds(pl.multiple_of(z * ROW, ROW), ROW), :]
    place = lax.broadcasted_iota(jnp.int32, widths.shape, 1) - WIDTH_AT
    query = lax.broadcasted_iota(jnp.int32, widths.shape, 0)
    offset = (r - query + NEAR) & (ROW - 1)
    group = z * ROW + query + offset - NEAR
    valid = (group >= 0) & (group < ROW * ROW) & (place == offset)
    step = (group >> 3) - z
    slot = jnp.where(step == 0, 0, jnp.where(step < 0, 1, 2))
    near = jnp.sum(jnp.where(valid, widths * 16 + slot, 0), axis=1, keepdims=True)
    near = jnp.concatenate((near, jnp.zeros((rows - ROW, 1), jnp.int32)), axis=0)
    table_ref[...] = jnp.where(lane == NEAR_AT, near, table)
    for copy in copies:
        copy.wait()


def three_parts(x):
    high = x.astype(jnp.bfloat16).astype(jnp.float32)
    rest = x - high
    middle = rest.astype(jnp.bfloat16).astype(jnp.float32)
    return [high, middle, rest - middle]


def two_parts(x):
    high = x.astype(jnp.bfloat16).astype(jnp.float32)
    return [high, x - high]


def list_units(table, first, count, units):
    def one_block(i, n):
        for s in range(count):
            asked = table[i, first + s]
            units[n] = i * 16 + s * 2 + asked - 1
            n = n + jnp.where(asked > 0, 1, 0)
        return n

    return lax.fori_loop(0, 2 * ROW, one_block, jnp.int32(0))


def set_text(tiles, table, bias, text_k, text_v):
    z = table[0, WHERE_AT]
    r = table[0, WHERE_AT + 1]
    row = lax.broadcasted_iota(jnp.int32, (TEXT_ROWS, 2 * BLK), 0)
    keys = []
    vals = []
    for s, step in enumerate(EARLY + LATE):
        first = (((z + step) & (ROW - 1)) * ROW + r) * 4
        alive = (row < 4) & (first + row < table[0, LEN_AT])
        bias[s * TEXT_ROWS : (s + 1) * TEXT_ROWS, :] = jnp.where(alive, 0.0, NEG)
        tile = tiles[s].astype(jnp.float32)[:TEXT_ROWS]
        keys.append(tile)
        vals.append(pltpu.roll(tile, 4, 0))
    text_k[...] = jnp.concatenate(keys, axis=0).astype(jnp.bfloat16)
    spare = HD - ROW * TEXT_ROWS
    vals.append(jnp.zeros((spare, 2 * HD), jnp.float32))
    vals = jnp.concatenate(vals, axis=0)
    for h in range(2):
        text_v[h] = vals[:, h * HD : (h + 1) * HD].T.astype(jnp.bfloat16)[:, : HD - spare]


def group_queries(q_ref, g, h):
    lanes = slice(h * HD, (h + 1) * HD)
    return jnp.concatenate((q_ref[g, :BLK, lanes], q_ref[g, BLK:, lanes]), axis=1)


def product(left, right):
    return jnp.dot(left, right, preferred_element_type=jnp.float32)


def head_rows(h):
    return slice(h * HD, (h + 1) * HD)


def text_step(q_ref, cases, text_k, text_v, bias):
    scores = [
        product(text_k[:, head_rows(h)], group_queries(q_ref, g, h)) * SCORE_SCALE + bias[...] for g, h in cases
    ]
    tops = [jnp.maximum(jnp.max(s, axis=0, keepdims=True), FLOOR) for s in scores]
    weights = [jnp.exp2(s - top) for s, top in zip(scores, tops)]
    totals = [jnp.sum(p, axis=0, keepdims=True) for p in weights]
    outs = [product(text_v[h], p.astype(jnp.bfloat16)) for (_, h), p in zip(cases, weights)]
    return list(zip(tops, totals, outs))


def group_cases(step, groups):
    return [(step * groups + j, h) for j in range(groups) for h in range(2)]


def joined(old, new):
    top = jnp.maximum(old[0], new[0])
    fade = jnp.exp2(old[0] - top)
    rise = jnp.exp2(new[0] - top)
    return top, old[1] * fade + new[1] * rise, old[2] * fade + new[2] * rise


def read_state(acc, stat, g, h):
    return stat[g, 2 * h : 2 * h + 1, :], stat[g, 2 * h + 1 : 2 * h + 2, :], acc[g, head_rows(h), :]


def write_state(acc, stat, g, h, state):
    stat[g, 2 * h : 2 * h + 1, :] = state[0]
    stat[g, 2 * h + 1 : 2 * h + 2, :] = state[1]
    acc[g, head_rows(h), :] = state[2]


def walk_units(units, count, q_ref, kv, acc, stat):
    def step(t, _):
        work = []
        for j in range(TOGETHER):
            number = t * TOGETHER + j
            code = jnp.where(number < count, units[number], 0)
            gone = jnp.where(number < count, 0.0, NEG)
            block = code >> 4
            g = block >> 1
            across = pl.multiple_of((block & 1) * BLK, BLK)
            who = (code & 15) >> 1
            down = pl.multiple_of((code & 1) * BLK, BLK)
            for h in range(2):
                s = product(
                    kv[who, pl.ds(down, BLK), head_rows(h)], q_ref[g, pl.ds(across, BLK), head_rows(h)]
                )
                work.append((g, across, who, down, h, gone, s * SCORE_SCALE))
        done = []
        for g, across, who, down, h, gone, s in work:
            top = jnp.max(s, axis=0, keepdims=True)
            p = jnp.exp2(s - top)
            total = jnp.sum(p, axis=0, keepdims=True)
            out = product(kv[who, pl.ds(down + 2 * BLK, BLK), head_rows(h)], p.astype(jnp.bfloat16))
            done.append((g, across, h, top + gone, total, out))
        for g, across, h, top, total, out in done:
            lanes = pl.ds(across, BLK)
            old_top = stat[g, 2 * h : 2 * h + 1, lanes]
            new_top = jnp.maximum(old_top, top)
            fade = jnp.exp2(old_top - new_top)
            rise = jnp.exp2(top - new_top)
            stat[g, 2 * h : 2 * h + 1, lanes] = new_top
            stat[g, 2 * h + 1 : 2 * h + 2, lanes] = (
                stat[g, 2 * h + 1 : 2 * h + 2, lanes] * fade + total * rise
            )
            acc[g, head_rows(h), lanes] = acc[g, head_rows(h), lanes] * fade + out * rise
        return 0

    lax.fori_loop(0, (count + TOGETHER - 1) // TOGETHER, step, 0)


def start_all(pairs, sems):
    copies = [pltpu.make_async_copy(src, dst, sems.at[i]) for i, (src, dst) in enumerate(pairs)]
    for copy in copies:
        copy.start()
    return [copy.wait for copy in copies]


def early_kernel(table, q_ref, own, f1, b1, f2, b2, acc, stat, kv, units, sems):
    waits = start_all([(x, kv.at[i]) for i, x in enumerate((own, f1, b1, f2, b2))], sems)
    count = list_units(table, 0, len(EARLY), units)
    for wait in waits:
        wait()
    offset = lax.broadcasted_iota(jnp.int32, (2 * BLK, 2 * BLK), 0) - lax.broadcasted_iota(
        jnp.int32, (2 * BLK, 2 * BLK), 1
    )
    distance = jnp.abs(offset)

    r = table[0, WHERE_AT + 1]
    for steps in ((0, 1), (2, 3), (4,)):
        cases = []
        for step in steps:
            g = (r + NEAR - step) & (ROW - 1)
            near = table[g, NEAR_AT]
            who = near & 15
            for h in range(2):
                s = product(kv[who, : 2 * BLK, head_rows(h)], group_queries(q_ref, g, h)) * SCORE_SCALE
                cases.append((g, h, who, jnp.where(distance < (near >> 4), s, NEG)))
        fresh = []
        for g, h, who, s in cases:
            top = jnp.maximum(jnp.max(s, axis=0, keepdims=True), FLOOR)
            p = jnp.exp2(s - top)
            values = jnp.concatenate(
                (kv[who, 2 * BLK : 3 * BLK, head_rows(h)], kv[who, 3 * BLK : 4 * BLK, head_rows(h)]), axis=1
            )
            out = product(values, p.astype(jnp.bfloat16))
            fresh.append((g, h, (top, jnp.sum(p, axis=0, keepdims=True), out)))
        for g, h, state in fresh:
            write_state(acc, stat, g, h, state)
            stat[g, 4:8, :] = jnp.zeros((4, 2 * BLK), jnp.float32)
    row = lax.broadcasted_iota(jnp.int32, (8, 2 * BLK), 0)
    for step in range(2 * NEAR + 1, ROW):
        g = (r + NEAR - step) & (ROW - 1)
        acc[g, :, :] = jnp.zeros((2 * HD, 2 * BLK), jnp.float32)
        stat[g, :, :] = jnp.where((row == 0) | (row == 2), FLOOR, 0.0)
    walk_units(units, count, q_ref, kv, acc, stat)


def late_kernel(
    table, q_ref, own, f1, b1, f2, b2, f3, b3, far4, acc_in, stat_in, out_ref, acc, stat,
    kv, units, sems, tiles, bias, text_k, text_v,
):
    pairs = [(f3, kv.at[0]), (b3, kv.at[1]), (far4, kv.at[2])]
    for i, x in enumerate((own, f1, b1, f2, b2, f3, b3, far4)):
        pairs.append((x.at[4 * BLK :], tiles.at[i]))
    waits = start_all(pairs, sems)
    count = list_units(table, len(EARLY), len(LATE), units)
    for wait in waits:
        wait()
    set_text(tiles, table, bias, text_k, text_v)
    walk_units(units, count, q_ref, kv, acc, stat)

    def some_groups(step, _):
        cases = group_cases(step, GROUPS_AT_ONCE)
        fresh = text_step(q_ref, cases, text_k, text_v, bias)
        done = [joined(read_state(acc, stat, g, h), new) for (g, h), new in zip(cases, fresh)]
        for x in range(0, len(cases), 2):
            g = cases[x][0]
            rows = []
            for h in range(2):
                top, total, out = done[x + h]
                out_ref[g, head_rows(h), :] = out.astype(jnp.bfloat16)
                rows += three_parts(top) + two_parts(total)
            rows.append(jnp.zeros((TPAD - len(rows), 2 * BLK), jnp.float32))
            out_ref[g, 2 * HD : 2 * HD + TPAD, :] = jnp.concatenate(rows, axis=0).astype(jnp.bfloat16)
        return 0

    lax.fori_loop(0, ROW // GROUPS_AT_ONCE, some_groups, 0)


def merge_kernel(part_ref, out_ref):
    stats = [part_ref[i, 2 * HD : 2 * HD + TPAD, :].astype(jnp.float32) for i in range(ROW)]
    for h in range(2):
        tops = [s[5 * h : 5 * h + 1] + s[5 * h + 1 : 5 * h + 2] + s[5 * h + 2 : 5 * h + 3] for s in stats]
        sums = [s[5 * h + 3 : 5 * h + 4] + s[5 * h + 4 : 5 * h + 5] for s in stats]
        top = functools.reduce(jnp.maximum, tops)
        weights = [jnp.exp2(t - top) for t in tops]
        total = functools.reduce(jnp.add, [w * s for w, s in zip(weights, sums)])
        inverse = 1.0 / total
        rows = slice(h * HD, (h + 1) * HD)
        acc = None
        for i in range(ROW):
            term = part_ref[i, rows, :].astype(jnp.float32) * weights[i]
            acc = term if acc is None else acc + term
        acc = (acc * inverse).astype(jnp.bfloat16)
        for i in range(ROW):
            out_ref[i, rows, :] = acc


def smem():
    return pl.BlockSpec(memory_space=pltpu.SMEM)


def vmem():
    return pl.BlockSpec(memory_space=pltpu.VMEM)


def anywhere():
    return pl.BlockSpec(memory_space=pl.ANY)


def kernel_params():
    return pltpu.CompilerParams(vmem_limit_bytes=32 << 20)


def attend_scratch(slots, copies):
    return [
        pltpu.VMEM((slots, MESSAGE, 2 * HD), jnp.bfloat16),
        pltpu.SMEM((2 * ROW * slots + 8,), jnp.int32),
        pltpu.SemaphoreType.DMA((copies,)),
    ]


def text_scratch():
    return [
        pltpu.VMEM((ROW, TPAD, 2 * HD), jnp.bfloat16),
        pltpu.VMEM((ROW * TEXT_ROWS, 2 * BLK), jnp.float32),
        pltpu.VMEM((ROW * TEXT_ROWS, 2 * HD), jnp.bfloat16),
        pltpu.VMEM((2, HD, ROW * TEXT_ROWS), jnp.bfloat16),
    ]


def shards(
    queries,
    keys,
    values,
    text_keys,
    text_values,
    text_len,
    radial_width,
    far_blocks,
    far_count,
    w_out,
):
    own = lax.axis_index("seq")
    where = jnp.stack((own // ROW, own % ROW, text_len[0])).astype(jnp.int32)
    tokens, width = queries.shape
    heads = lax.axis_size("head")
    columns = w_out.shape[1] // heads

    whole = pltpu.CompilerParams(vmem_limit_bytes=60 << 20)
    kv, q_mine = pl.pallas_call(
        message_kernel,
        out_shape=(
            jax.ShapeDtypeStruct((MESSAGE, width), jnp.bfloat16),
            jax.ShapeDtypeStruct((ROW, tokens, width), jnp.bfloat16),
        ),
        in_specs=[anywhere()] * 3 + [vmem()] * 2,
        out_specs=(vmem(), vmem()),
        scratch_shapes=[
            pltpu.VMEM((tokens, width), jnp.bfloat16),
            pltpu.VMEM((tokens, width), jnp.bfloat16),
            pltpu.SemaphoreType.DMA((3,)),
        ],
        compiler_params=whole,
        name="messages",
    )(keys, values, queries, text_keys, text_values)
    table, quarter = pl.pallas_call(
        list_kernel,
        out_shape=(
            jax.ShapeDtypeStruct((2 * ROW, BLK), jnp.int32),
            jax.ShapeDtypeStruct((heads, width // 4, columns), jnp.bfloat16),
        ),
        in_specs=[smem(), vmem(), vmem(), vmem(), anywhere()],
        out_specs=(vmem(), vmem()),
        scratch_shapes=[
            pltpu.VMEM((BLK, BLK), jnp.int32),
            pltpu.VMEM((BLK, BLK), jnp.int32),
            pltpu.SemaphoreType.DMA((heads,)),
        ],
        compiler_params=whole,
        cost_estimate=pl.CostEstimate(flops=40 * 10**9, bytes_accessed=10**5, transcendentals=0),
        name="lists",
    )(where, far_blocks.T, far_count[None, :], radial_width.T, w_out)

    count = ROW * ROW
    later, table = lax.optimization_barrier((kv, table))
    f1 = along_column(later, 1)
    b1 = along_column(later, -1)
    q_all = lax.all_to_all(q_mine, "seq", 0, 0, axis_index_groups=row_peers())
    f2 = along_column(kv, 2)
    b2 = along_column(kv, -2)
    f2, b2, table, quarter = lax.optimization_barrier((f2, b2, table, quarter))
    f3 = along_column(f2, 1)
    b3 = along_column(b2, -1)
    far4 = lax.ppermute(
        jnp.where(own % 2 == 0, f2, b2),
        "seq",
        [(g, (g + (2 * ROW if g % 2 == 0 else -2 * ROW)) % count) for g in range(count)],
    )
    quarter, q_all = lax.optimization_barrier((quarter, q_all))
    quarter = lax.all_to_all(quarter, "head", 0, 0)

    acc, stat = pl.pallas_call(
        early_kernel,
        out_shape=(
            jax.ShapeDtypeStruct((ROW, width, tokens), jnp.float32),
            jax.ShapeDtypeStruct((ROW, 8, tokens), jnp.float32),
        ),
        in_specs=[smem(), vmem()] + [anywhere()] * 5,
        out_specs=(vmem(), vmem()),
        scratch_shapes=attend_scratch(len(EARLY), 5),
        compiler_params=kernel_params(),
        cost_estimate=pl.CostEstimate(flops=6 * 10**9, bytes_accessed=5 * 10**6, transcendentals=0),
        name="attend_early",
    )(table, q_all, kv, f1, b1, f2, b2)
    part, _, _ = pl.pallas_call(
        late_kernel,
        out_shape=(
            jax.ShapeDtypeStruct((ROW, width + TPAD, tokens), jnp.bfloat16),
            jax.ShapeDtypeStruct(acc.shape, acc.dtype),
            jax.ShapeDtypeStruct(stat.shape, stat.dtype),
        ),
        in_specs=[smem(), vmem()] + [anywhere()] * 8 + [vmem()] * 2,
        out_specs=(vmem(),) * 3,
        scratch_shapes=attend_scratch(len(LATE), 3 + ROW) + text_scratch(),
        input_output_aliases={10: 1, 11: 2},
        compiler_params=kernel_params(),
        cost_estimate=pl.CostEstimate(flops=4 * 10**9, bytes_accessed=5 * 10**6, transcendentals=0),
        name="attend_late",
    )(table, q_all, kv, f1, b1, f2, b2, f3, b3, far4, acc, stat)
    part, quarter = lax.optimization_barrier((part, quarter))
    part = lax.all_to_all(part, "seq", 0, 0, axis_index_groups=row_peers())
    low = (own & ROW) == 0
    other = lax.ppermute(quarter, "seq", [(g, g ^ ROW) for g in range(count)])
    halves = jnp.stack((jnp.where(low, quarter, other), jnp.where(low, other, quarter)), axis=1)
    theirs = lax.ppermute(halves, "seq", [(g, g ^ 1) for g in range(count)])
    even = (own & 1) == 0
    w_mine = jnp.stack((jnp.where(even, halves, theirs), jnp.where(even, theirs, halves)), axis=2)
    merged = pl.pallas_call(
        merge_kernel,
        out_shape=jax.ShapeDtypeStruct((ROW, width, tokens), jnp.bfloat16),
        in_specs=[vmem()],
        out_specs=vmem(),
        compiler_params=kernel_params(),
        name="merge",
    )(part)
    attention = lax.all_to_all(merged, "head", 0, 0)
    mixed = lax.dot_general(
        attention.reshape(heads * width, tokens),
        w_mine.reshape(heads * width, columns),
        (((0,), (0,)), ((), ())),
        preferred_element_type=jnp.float32,
    )
    return mixed.astype(jnp.bfloat16)


def solution(mesh):
    return jax.shard_map(
        shards,
        mesh=mesh,
        in_specs=(
            P("seq", "head"),
            P("seq", "head"),
            P("seq", "head"),
            P("seq", "head"),
            P("seq", "head"),
            P(),
            P(),
            P(),
            P(),
            P("head", None),
        ),
        out_specs=P("seq", "head"),
        check_vma=False,
    )
```

```python
import functools

import jax
import jax.numpy as jnp
from jax import lax
from jax.experimental import pallas as pl
from jax.experimental.pallas import tpu as pltpu
from jax.sharding import PartitionSpec as P

HD = 128
BLK = 128
NEAR = 2
ROW = 8
TPAD = 16
NEG = -1e30
FLOOR = -1e9
SCORE_SCALE = HD ** (-0.5) * 1.4426950408889634
EARLY = (0, -1, 1, -2, 2)
LATE = (-3, 3, 4)
TOGETHER = 8
TEXT_ROWS = 8
GROUPS_AT_ONCE = 8
MESSAGE = 4 * BLK + TPAD
NEAR_AT = ROW
COUNT_AT = 32
WIDTH_AT = 40
LEN_AT = ROW + 1
WHERE_AT = ROW + 2


def row_peers():
    return [[z * ROW + r for r in range(ROW)] for z in range(ROW)]


def along_column(block, distance):
    count = ROW * ROW
    return lax.ppermute(block, "seq", [(g, (g + ROW * distance) % count) for g in range(count)])


def turned(buf):
    for a in range(2):
        for h in range(2):
            tile = buf[a * BLK : (a + 1) * BLK, h * HD : (h + 1) * HD].astype(jnp.float32)
            yield a, h, tile.T.astype(jnp.bfloat16)


def message_kernel(k_in, v_in, q_in, tk_in, tv_in, kv_out, q_out, v_buf, q_buf, sems):
    copies = [
        pltpu.make_async_copy(v_in, v_buf, sems.at[0]),
        pltpu.make_async_copy(q_in, q_buf, sems.at[1]),
        pltpu.make_async_copy(k_in, kv_out.at[: 2 * BLK], sems.at[2]),
    ]
    for copy in copies:
        copy.start()
    blank = jnp.zeros((TPAD - 2 * tk_in.shape[0], kv_out.shape[1]), jnp.float32)
    text = (tk_in[...].astype(jnp.float32), tv_in[...].astype(jnp.float32), blank)
    kv_out[4 * BLK :, :] = jnp.concatenate(text, axis=0).astype(jnp.bfloat16)
    copies[0].wait()
    for a, h, tile in turned(v_buf):
        kv_out[(2 + a) * BLK : (3 + a) * BLK, h * HD : (h + 1) * HD] = tile
    copies[1].wait()
    for a, h, tile in turned(q_buf):
        for i in range(ROW):
            q_out[i, a * BLK : (a + 1) * BLK, h * HD : (h + 1) * HD] = tile
    copies[2].wait()


def list_kernel(where_ref, far_ref, count_ref, width_ref, w_in, table_ref, w_out, wide, tall, sems):
    z = where_ref[0]
    r = where_ref[1]
    heads, quarter, columns = w_out.shape
    start = pl.multiple_of(((z & 1) * 2 + (r & 1)) * quarter, quarter)
    copies = [
        pltpu.make_async_copy(
            w_in.at[pl.ds(start, quarter), i * columns : (i + 1) * columns], w_out.at[i], sems.at[i]
        )
        for i in range(heads)
    ]
    for copy in copies:
        copy.start()
    rows = 2 * ROW
    slots = far_ref.shape[0]
    wide[...] = jnp.zeros(wide.shape, jnp.int32)
    wide[:slots, :] = far_ref[...]
    wide[COUNT_AT : COUNT_AT + 1, :] = count_ref[...]
    wide[WIDTH_AT : WIDTH_AT + 2 * NEAR + 1, : ROW * ROW] = width_ref[...]
    tall[...] = wide[...].T
    mine = tall[pl.ds(pl.multiple_of(z * rows, rows), rows), :]
    place = lax.broadcasted_iota(jnp.int32, mine.shape, 1)
    count = jnp.sum(jnp.where(place == COUNT_AT, mine, 0), axis=1, keepdims=True)
    live = (place < count) & (place < slots)
    lane = lax.broadcasted_iota(jnp.int32, (rows, BLK), 1)
    table = jnp.where(lane == LEN_AT, where_ref[2], 0)
    table = jnp.where(lane == WHERE_AT, z, table)
    table = jnp.where(lane == WHERE_AT + 1, r, table)
    for s, step in enumerate(EARLY + LATE):
        group = ((z + step) & (ROW - 1)) * ROW + r
        asked = jnp.where(live & ((mine >> 1) == group), 1 + (mine & 1), 0)
        table = jnp.where(lane == s, jnp.sum(asked, axis=1, keepdims=True), table)
    widths = tall[pl.ds(pl.multiple_of(z * ROW, ROW), ROW), :]
    place = lax.broadcasted_iota(jnp.int32, widths.shape, 1) - WIDTH_AT
    query = lax.broadcasted_iota(jnp.int32, widths.shape, 0)
    offset = (r - query + NEAR) & (ROW - 1)
    group = z * ROW + query + offset - NEAR
    valid = (group >= 0) & (group < ROW * ROW) & (place == offset)
    step = (group >> 3) - z
    slot = jnp.where(step == 0, 0, jnp.where(step < 0, 1, 2))
    near = jnp.sum(jnp.where(valid, widths * 16 + slot, 0), axis=1, keepdims=True)
    near = jnp.concatenate((near, jnp.zeros((rows - ROW, 1), jnp.int32)), axis=0)
    table_ref[...] = jnp.where(lane == NEAR_AT, near, table)
    for copy in copies:
        copy.wait()


def three_parts(x):
    high = x.astype(jnp.bfloat16).astype(jnp.float32)
    rest = x - high
    middle = rest.astype(jnp.bfloat16).astype(jnp.float32)
    return [high, middle, rest - middle]


def two_parts(x):
    high = x.astype(jnp.bfloat16).astype(jnp.float32)
    return [high, x - high]


def list_units(table, first, count, units):
    def one_block(i, n):
        for s in range(count):
            asked = table[i, first + s]
            units[n] = i * 16 + s * 2 + asked - 1
            n = n + jnp.where(asked > 0, 1, 0)
        return n

    return lax.fori_loop(0, 2 * ROW, one_block, jnp.int32(0))


def set_text(tiles, table, bias, text_k, text_v):
    z = table[0, WHERE_AT]
    r = table[0, WHERE_AT + 1]
    row = lax.broadcasted_iota(jnp.int32, (TEXT_ROWS, 2 * BLK), 0)
    keys = []
    vals = []
    for s, step in enumerate(EARLY + LATE):
        first = (((z + step) & (ROW - 1)) * ROW + r) * 4
        alive = (row < 4) & (first + row < table[0, LEN_AT])
        bias[s * TEXT_ROWS : (s + 1) * TEXT_ROWS, :] = jnp.where(alive, 0.0, NEG)
        tile = tiles[s].astype(jnp.float32)[:TEXT_ROWS]
        keys.append(tile)
        vals.append(pltpu.roll(tile, 4, 0))
    text_k[...] = jnp.concatenate(keys, axis=0).astype(jnp.bfloat16)
    spare = HD - ROW * TEXT_ROWS
    vals.append(jnp.zeros((spare, 2 * HD), jnp.float32))
    vals = jnp.concatenate(vals, axis=0)
    for h in range(2):
        text_v[h] = vals[:, h * HD : (h + 1) * HD].T.astype(jnp.bfloat16)[:, : HD - spare]


def group_queries(q_ref, g, h):
    lanes = slice(h * HD, (h + 1) * HD)
    return jnp.concatenate((q_ref[g, :BLK, lanes], q_ref[g, BLK:, lanes]), axis=1)


def product(left, right):
    return jnp.dot(left, right, preferred_element_type=jnp.float32)


def head_rows(h):
    return slice(h * HD, (h + 1) * HD)


def text_step(q_ref, cases, text_k, text_v, bias):
    scores = [
        product(text_k[:, head_rows(h)], group_queries(q_ref, g, h)) * SCORE_SCALE + bias[...] for g, h in cases
    ]
    tops = [jnp.maximum(jnp.max(s, axis=0, keepdims=True), FLOOR) for s in scores]
    weights = [jnp.exp2(s - top) for s, top in zip(scores, tops)]
    totals = [jnp.sum(p, axis=0, keepdims=True) for p in weights]
    outs = [product(text_v[h], p.astype(jnp.bfloat16)) for (_, h), p in zip(cases, weights)]
    return list(zip(tops, totals, outs))


def group_cases(step, groups):
    return [(step * groups + j, h) for j in range(groups) for h in range(2)]


def joined(old, new):
    top = jnp.maximum(old[0], new[0])
    fade = jnp.exp2(old[0] - top)
    rise = jnp.exp2(new[0] - top)
    return top, old[1] * fade + new[1] * rise, old[2] * fade + new[2] * rise


def read_state(acc, stat, g, h):
    return stat[g, 2 * h : 2 * h + 1, :], stat[g, 2 * h + 1 : 2 * h + 2, :], acc[g, head_rows(h), :]


def write_state(acc, stat, g, h, state):
    stat[g, 2 * h : 2 * h + 1, :] = state[0]
    stat[g, 2 * h + 1 : 2 * h + 2, :] = state[1]
    acc[g, head_rows(h), :] = state[2]


def walk_units(units, count, q_ref, kv, acc, stat):
    def step(t, _):
        work = []
        for j in range(TOGETHER):
            number = t * TOGETHER + j
            code = jnp.where(number < count, units[number], 0)
            gone = jnp.where(number < count, 0.0, NEG)
            block = code >> 4
            g = block >> 1
            across = pl.multiple_of((block & 1) * BLK, BLK)
            who = (code & 15) >> 1
            down = pl.multiple_of((code & 1) * BLK, BLK)
            for h in range(2):
                s = product(
                    kv[who, pl.ds(down, BLK), head_rows(h)], q_ref[g, pl.ds(across, BLK), head_rows(h)]
                )
                work.append((g, across, who, down, h, gone, s * SCORE_SCALE))
        done = []
        for g, across, who, down, h, gone, s in work:
            top = jnp.max(s, axis=0, keepdims=True)
            p = jnp.exp2(s - top)
            total = jnp.sum(p, axis=0, keepdims=True)
            out = product(kv[who, pl.ds(down + 2 * BLK, BLK), head_rows(h)], p.astype(jnp.bfloat16))
            done.append((g, across, h, top + gone, total, out))
        for g, across, h, top, total, out in done:
            lanes = pl.ds(across, BLK)
            old_top = stat[g, 2 * h : 2 * h + 1, lanes]
            new_top = jnp.maximum(old_top, top)
            fade = jnp.exp2(old_top - new_top)
            rise = jnp.exp2(top - new_top)
            stat[g, 2 * h : 2 * h + 1, lanes] = new_top
            stat[g, 2 * h + 1 : 2 * h + 2, lanes] = (
                stat[g, 2 * h + 1 : 2 * h + 2, lanes] * fade + total * rise
            )
            acc[g, head_rows(h), lanes] = acc[g, head_rows(h), lanes] * fade + out * rise
        return 0

    lax.fori_loop(0, (count + TOGETHER - 1) // TOGETHER, step, 0)


def start_all(pairs, sems):
    copies = [pltpu.make_async_copy(src, dst, sems.at[i]) for i, (src, dst) in enumerate(pairs)]
    for copy in copies:
        copy.start()
    return [copy.wait for copy in copies]


def early_kernel(table, q_ref, own, f1, b1, f2, b2, acc, stat, kv, units, sems):
    waits = start_all([(x, kv.at[i]) for i, x in enumerate((own, f1, b1, f2, b2))], sems)
    count = list_units(table, 0, len(EARLY), units)
    for wait in waits:
        wait()
    offset = lax.broadcasted_iota(jnp.int32, (2 * BLK, 2 * BLK), 0) - lax.broadcasted_iota(
        jnp.int32, (2 * BLK, 2 * BLK), 1
    )
    distance = jnp.abs(offset)

    r = table[0, WHERE_AT + 1]
    for steps in ((0, 1), (2, 3), (4,)):
        cases = []
        for step in steps:
            g = (r + NEAR - step) & (ROW - 1)
            near = table[g, NEAR_AT]
            who = near & 15
            for h in range(2):
                s = product(kv[who, : 2 * BLK, head_rows(h)], group_queries(q_ref, g, h)) * SCORE_SCALE
                cases.append((g, h, who, jnp.where(distance < (near >> 4), s, NEG)))
        fresh = []
        for g, h, who, s in cases:
            top = jnp.maximum(jnp.max(s, axis=0, keepdims=True), FLOOR)
            p = jnp.exp2(s - top)
            values = jnp.concatenate(
                (kv[who, 2 * BLK : 3 * BLK, head_rows(h)], kv[who, 3 * BLK : 4 * BLK, head_rows(h)]), axis=1
            )
            out = product(values, p.astype(jnp.bfloat16))
            fresh.append((g, h, (top, jnp.sum(p, axis=0, keepdims=True), out)))
        for g, h, state in fresh:
            write_state(acc, stat, g, h, state)
            stat[g, 4:8, :] = jnp.zeros((4, 2 * BLK), jnp.float32)
    row = lax.broadcasted_iota(jnp.int32, (8, 2 * BLK), 0)
    for step in range(2 * NEAR + 1, ROW):
        g = (r + NEAR - step) & (ROW - 1)
        acc[g, :, :] = jnp.zeros((2 * HD, 2 * BLK), jnp.float32)
        stat[g, :, :] = jnp.where((row == 0) | (row == 2), FLOOR, 0.0)
    walk_units(units, count, q_ref, kv, acc, stat)


def late_kernel(
    table, q_ref, own, f1, b1, f2, b2, f3, b3, far4, acc_in, stat_in, out_ref, acc, stat,
    kv, units, sems, tiles, bias, text_k, text_v,
):
    pairs = [(f3, kv.at[0]), (b3, kv.at[1]), (far4, kv.at[2])]
    for i, x in enumerate((own, f1, b1, f2, b2, f3, b3, far4)):
        pairs.append((x.at[4 * BLK :], tiles.at[i]))
    waits = start_all(pairs, sems)
    count = list_units(table, len(EARLY), len(LATE), units)
    for wait in waits:
        wait()
    set_text(tiles, table, bias, text_k, text_v)
    walk_units(units, count, q_ref, kv, acc, stat)

    def some_groups(step, _):
        cases = group_cases(step, GROUPS_AT_ONCE)
        fresh = text_step(q_ref, cases, text_k, text_v, bias)
        done = [joined(read_state(acc, stat, g, h), new) for (g, h), new in zip(cases, fresh)]
        for x in range(0, len(cases), 2):
            g = cases[x][0]
            rows = []
            for h in range(2):
                top, total, out = done[x + h]
                out_ref[g, head_rows(h), :] = out.astype(jnp.bfloat16)
                rows += three_parts(top) + two_parts(total)
            rows.append(jnp.zeros((TPAD - len(rows), 2 * BLK), jnp.float32))
            out_ref[g, 2 * HD : 2 * HD + TPAD, :] = jnp.concatenate(rows, axis=0).astype(jnp.bfloat16)
        return 0

    lax.fori_loop(0, ROW // GROUPS_AT_ONCE, some_groups, 0)


def merge_kernel(part_ref, out_ref):
    stats = [part_ref[i, 2 * HD : 2 * HD + TPAD, :].astype(jnp.float32) for i in range(ROW)]
    for h in range(2):
        tops = [s[5 * h : 5 * h + 1] + s[5 * h + 1 : 5 * h + 2] + s[5 * h + 2 : 5 * h + 3] for s in stats]
        sums = [s[5 * h + 3 : 5 * h + 4] + s[5 * h + 4 : 5 * h + 5] for s in stats]
        top = functools.reduce(jnp.maximum, tops)
        weights = [jnp.exp2(t - top) for t in tops]
        total = functools.reduce(jnp.add, [w * s for w, s in zip(weights, sums)])
        inverse = 1.0 / total
        rows = slice(h * HD, (h + 1) * HD)
        acc = None
        for i in range(ROW):
            term = part_ref[i, rows, :].astype(jnp.float32) * weights[i]
            acc = term if acc is None else acc + term
        acc = (acc * inverse).astype(jnp.bfloat16)
        for i in range(ROW):
            out_ref[i, rows, :] = acc


def smem():
    return pl.BlockSpec(memory_space=pltpu.SMEM)


def vmem():
    return pl.BlockSpec(memory_space=pltpu.VMEM)


def anywhere():
    return pl.BlockSpec(memory_space=pl.ANY)


def kernel_params():
    return pltpu.CompilerParams(vmem_limit_bytes=32 << 20)


def attend_scratch(slots, copies):
    return [
        pltpu.VMEM((slots, MESSAGE, 2 * HD), jnp.bfloat16),
        pltpu.SMEM((2 * ROW * slots + 8,), jnp.int32),
        pltpu.SemaphoreType.DMA((copies,)),
    ]


def text_scratch():
    return [
        pltpu.VMEM((ROW, TPAD, 2 * HD), jnp.bfloat16),
        pltpu.VMEM((ROW * TEXT_ROWS, 2 * BLK), jnp.float32),
        pltpu.VMEM((ROW * TEXT_ROWS, 2 * HD), jnp.bfloat16),
        pltpu.VMEM((2, HD, ROW * TEXT_ROWS), jnp.bfloat16),
    ]


def shards(
    queries,
    keys,
    values,
    text_keys,
    text_values,
    text_len,
    radial_width,
    far_blocks,
    far_count,
    w_out,
):
    own = lax.axis_index("seq")
    where = jnp.stack((own // ROW, own % ROW, text_len[0])).astype(jnp.int32)
    tokens, width = queries.shape
    heads = lax.axis_size("head")
    columns = w_out.shape[1] // heads

    whole = pltpu.CompilerParams(vmem_limit_bytes=60 << 20)
    kv, q_mine = pl.pallas_call(
        message_kernel,
        out_shape=(
            jax.ShapeDtypeStruct((MESSAGE, width), jnp.bfloat16),
            jax.ShapeDtypeStruct((ROW, tokens, width), jnp.bfloat16),
        ),
        in_specs=[anywhere()] * 3 + [vmem()] * 2,
        out_specs=(vmem(), vmem()),
        scratch_shapes=[
            pltpu.VMEM((tokens, width), jnp.bfloat16),
            pltpu.VMEM((tokens, width), jnp.bfloat16),
            pltpu.SemaphoreType.DMA((3,)),
        ],
        compiler_params=whole,
        name="messages",
    )(keys, values, queries, text_keys, text_values)
    table, quarter = pl.pallas_call(
        list_kernel,
        out_shape=(
            jax.ShapeDtypeStruct((2 * ROW, BLK), jnp.int32),
            jax.ShapeDtypeStruct((heads, width // 4, columns), jnp.bfloat16),
        ),
        in_specs=[smem(), vmem(), vmem(), vmem(), anywhere()],
        out_specs=(vmem(), vmem()),
        scratch_shapes=[
            pltpu.VMEM((BLK, BLK), jnp.int32),
            pltpu.VMEM((BLK, BLK), jnp.int32),
            pltpu.SemaphoreType.DMA((heads,)),
        ],
        compiler_params=whole,
        cost_estimate=pl.CostEstimate(flops=40 * 10**9, bytes_accessed=10**5, transcendentals=0),
        name="lists",
    )(where, far_blocks.T, far_count[None, :], radial_width.T, w_out)

    count = ROW * ROW
    later, table = lax.optimization_barrier((kv, table))
    f1 = along_column(later, 1)
    b1 = along_column(later, -1)
    q_all = lax.all_to_all(q_mine, "seq", 0, 0, axis_index_groups=row_peers())
    f2 = along_column(kv, 2)
    b2 = along_column(kv, -2)
    f2, b2, table, quarter = lax.optimization_barrier((f2, b2, table, quarter))
    f3 = along_column(f2, 1)
    b3 = along_column(b2, -1)
    far4 = lax.ppermute(
        later, "seq", [(g, (g + (4 * ROW if g % 2 == 0 else -4 * ROW)) % count) for g in range(count)]
    )
    quarter, q_all = lax.optimization_barrier((quarter, q_all))
    quarter = lax.all_to_all(quarter, "head", 0, 0)

    acc, stat = pl.pallas_call(
        early_kernel,
        out_shape=(
            jax.ShapeDtypeStruct((ROW, width, tokens), jnp.float32),
            jax.ShapeDtypeStruct((ROW, 8, tokens), jnp.float32),
        ),
        in_specs=[smem(), vmem()] + [anywhere()] * 5,
        out_specs=(vmem(), vmem()),
        scratch_shapes=attend_scratch(len(EARLY), 5),
        compiler_params=kernel_params(),
        cost_estimate=pl.CostEstimate(flops=6 * 10**9, bytes_accessed=5 * 10**6, transcendentals=0),
        name="attend_early",
    )(table, q_all, kv, f1, b1, f2, b2)
    part, _, _ = pl.pallas_call(
        late_kernel,
        out_shape=(
            jax.ShapeDtypeStruct((ROW, width + TPAD, tokens), jnp.bfloat16),
            jax.ShapeDtypeStruct(acc.shape, acc.dtype),
            jax.ShapeDtypeStruct(stat.shape, stat.dtype),
        ),
        in_specs=[smem(), vmem()] + [anywhere()] * 8 + [vmem()] * 2,
        out_specs=(vmem(),) * 3,
        scratch_shapes=attend_scratch(len(LATE), 3 + ROW) + text_scratch(),
        input_output_aliases={10: 1, 11: 2},
        compiler_params=kernel_params(),
        cost_estimate=pl.CostEstimate(flops=4 * 10**9, bytes_accessed=5 * 10**6, transcendentals=0),
        name="attend_late",
    )(table, q_all, kv, f1, b1, f2, b2, f3, b3, far4, acc, stat)
    part, quarter = lax.optimization_barrier((part, quarter))
    part = lax.all_to_all(part, "seq", 0, 0, axis_index_groups=row_peers())
    low = (own & ROW) == 0
    other = lax.ppermute(quarter, "seq", [(g, g ^ ROW) for g in range(count)])
    halves = jnp.stack((jnp.where(low, quarter, other), jnp.where(low, other, quarter)), axis=1)
    theirs = lax.ppermute(halves, "seq", [(g, g ^ 1) for g in range(count)])
    even = (own & 1) == 0
    w_mine = jnp.stack((jnp.where(even, halves, theirs), jnp.where(even, theirs, halves)), axis=2)
    merged = pl.pallas_call(
        merge_kernel,
        out_shape=jax.ShapeDtypeStruct((ROW, width, tokens), jnp.bfloat16),
        in_specs=[vmem()],
        out_specs=vmem(),
        compiler_params=kernel_params(),
        name="merge",
    )(part)
    attention = lax.all_to_all(merged, "head", 0, 0)
    mixed = lax.dot_general(
        attention.reshape(heads * width, tokens),
        w_mine.reshape(heads * width, columns),
        (((0,), (0,)), ((), ())),
        preferred_element_type=jnp.float32,
    )
    return mixed.astype(jnp.bfloat16)


def solution(mesh):
    return jax.shard_map(
        shards,
        mesh=mesh,
        in_specs=(
            P("seq", "head"),
            P("seq", "head"),
            P("seq", "head"),
            P("seq", "head"),
            P("seq", "head"),
            P(),
            P(),
            P(),
            P(),
            P("head", None),
        ),
        out_specs=P("seq", "head"),
        check_vma=False,
    )
```

```python
import functools

import jax
import jax.numpy as jnp
from jax import lax
from jax.experimental import pallas as pl
from jax.experimental.pallas import tpu as pltpu
from jax.sharding import PartitionSpec as P

HD = 128
BLK = 128
NEAR = 2
ROW = 8
TPAD = 16
NEG = -1e30
FLOOR = -1e9
SCORE_SCALE = HD ** (-0.5) * 1.4426950408889634
EARLY = (0, -1, 1, -2, 2)
LATE = (-3, 3, 4)
TOGETHER = 8
TEXT_ROWS = 8
GROUPS_AT_ONCE = 8
MESSAGE = 4 * BLK + TPAD
NEAR_AT = ROW
COUNT_AT = 32
WIDTH_AT = 40
LEN_AT = ROW + 1
WHERE_AT = ROW + 2


def row_peers():
    return [[z * ROW + r for r in range(ROW)] for z in range(ROW)]


def along_column(block, distance):
    count = ROW * ROW
    return lax.ppermute(block, "seq", [(g, (g + ROW * distance) % count) for g in range(count)])


def turned(buf):
    for a in range(2):
        for h in range(2):
            tile = buf[a * BLK : (a + 1) * BLK, h * HD : (h + 1) * HD].astype(jnp.float32)
            yield a, h, tile.T.astype(jnp.bfloat16)


def message_kernel(k_in, v_in, q_in, tk_in, tv_in, kv_out, q_out, v_buf, q_buf, sems):
    copies = [
        pltpu.make_async_copy(v_in, v_buf, sems.at[0]),
        pltpu.make_async_copy(q_in, q_buf, sems.at[1]),
        pltpu.make_async_copy(k_in, kv_out.at[: 2 * BLK], sems.at[2]),
    ]
    for copy in copies:
        copy.start()
    blank = jnp.zeros((TPAD - 2 * tk_in.shape[0], kv_out.shape[1]), jnp.float32)
    text = (tk_in[...].astype(jnp.float32), tv_in[...].astype(jnp.float32), blank)
    kv_out[4 * BLK :, :] = jnp.concatenate(text, axis=0).astype(jnp.bfloat16)
    copies[0].wait()
    for a, h, tile in turned(v_buf):
        kv_out[(2 + a) * BLK : (3 + a) * BLK, h * HD : (h + 1) * HD] = tile
    copies[1].wait()
    for a, h, tile in turned(q_buf):
        for i in range(ROW):
            q_out[i, a * BLK : (a + 1) * BLK, h * HD : (h + 1) * HD] = tile
    copies[2].wait()


def list_kernel(where_ref, far_ref, count_ref, width_ref, w_in, table_ref, w_out, wide, tall, sems):
    z = where_ref[0]
    r = where_ref[1]
    heads, quarter, columns = w_out.shape
    start = pl.multiple_of(((z & 1) * 2 + (r & 1)) * quarter, quarter)
    copies = [
        pltpu.make_async_copy(
            w_in.at[pl.ds(start, quarter), i * columns : (i + 1) * columns], w_out.at[i], sems.at[i]
        )
        for i in range(heads)
    ]
    for copy in copies:
        copy.start()
    rows = 2 * ROW
    slots = far_ref.shape[0]
    wide[...] = jnp.zeros(wide.shape, jnp.int32)
    wide[:slots, :] = far_ref[...]
    wide[COUNT_AT : COUNT_AT + 1, :] = count_ref[...]
    wide[WIDTH_AT : WIDTH_AT + 2 * NEAR + 1, : ROW * ROW] = width_ref[...]
    tall[...] = wide[...].T
    mine = tall[pl.ds(pl.multiple_of(z * rows, rows), rows), :]
    place = lax.broadcasted_iota(jnp.int32, mine.shape, 1)
    count = jnp.sum(jnp.where(place == COUNT_AT, mine, 0), axis=1, keepdims=True)
    live = (place < count) & (place < slots)
    lane = lax.broadcasted_iota(jnp.int32, (rows, BLK), 1)
    table = jnp.where(lane == LEN_AT, where_ref[2], 0)
    table = jnp.where(lane == WHERE_AT, z, table)
    table = jnp.where(lane == WHERE_AT + 1, r, table)
    for s, step in enumerate(EARLY + LATE):
        group = ((z + step) & (ROW - 1)) * ROW + r
        asked = jnp.where(live & ((mine >> 1) == group), 1 + (mine & 1), 0)
        table = jnp.where(lane == s, jnp.sum(asked, axis=1, keepdims=True), table)
    widths = tall[pl.ds(pl.multiple_of(z * ROW, ROW), ROW), :]
    place = lax.broadcasted_iota(jnp.int32, widths.shape, 1) - WIDTH_AT
    query = lax.broadcasted_iota(jnp.int32, widths.shape, 0)
    offset = (r - query + NEAR) & (ROW - 1)
    group = z * ROW + query + offset - NEAR
    valid = (group >= 0) & (group < ROW * ROW) & (place == offset)
    step = (group >> 3) - z
    slot = jnp.where(step == 0, 0, jnp.where(step < 0, 1, 2))
    near = jnp.sum(jnp.where(valid, widths * 16 + slot, 0), axis=1, keepdims=True)
    near = jnp.concatenate((near, jnp.zeros((rows - ROW, 1), jnp.int32)), axis=0)
    table_ref[...] = jnp.where(lane == NEAR_AT, near, table)
    for copy in copies:
        copy.wait()


def three_parts(x):
    high = x.astype(jnp.bfloat16).astype(jnp.float32)
    rest = x - high
    middle = rest.astype(jnp.bfloat16).astype(jnp.float32)
    return [high, middle, rest - middle]


def two_parts(x):
    high = x.astype(jnp.bfloat16).astype(jnp.float32)
    return [high, x - high]


def list_units(table, first, count, units):
    def one_block(i, n):
        for s in range(count):
            asked = table[i, first + s]
            units[n] = i * 16 + s * 2 + asked - 1
            n = n + jnp.where(asked > 0, 1, 0)
        return n

    return lax.fori_loop(0, 2 * ROW, one_block, jnp.int32(0))


def set_text(tiles, table, bias, text_k, text_v):
    z = table[0, WHERE_AT]
    r = table[0, WHERE_AT + 1]
    row = lax.broadcasted_iota(jnp.int32, (TEXT_ROWS, 2 * BLK), 0)
    keys = []
    vals = []
    for s, step in enumerate(EARLY + LATE):
        first = (((z + step) & (ROW - 1)) * ROW + r) * 4
        alive = (row < 4) & (first + row < table[0, LEN_AT])
        bias[s * TEXT_ROWS : (s + 1) * TEXT_ROWS, :] = jnp.where(alive, 0.0, NEG)
        tile = tiles[s].astype(jnp.float32)[:TEXT_ROWS]
        keys.append(tile)
        vals.append(pltpu.roll(tile, 4, 0))
    text_k[...] = jnp.concatenate(keys, axis=0).astype(jnp.bfloat16)
    spare = HD - ROW * TEXT_ROWS
    vals.append(jnp.zeros((spare, 2 * HD), jnp.float32))
    vals = jnp.concatenate(vals, axis=0)
    for h in range(2):
        text_v[h] = vals[:, h * HD : (h + 1) * HD].T.astype(jnp.bfloat16)[:, : HD - spare]


def group_queries(q_ref, g, h):
    lanes = slice(h * HD, (h + 1) * HD)
    return jnp.concatenate((q_ref[g, :BLK, lanes], q_ref[g, BLK:, lanes]), axis=1)


def product(left, right):
    return jnp.dot(left, right, preferred_element_type=jnp.float32)


def head_rows(h):
    return slice(h * HD, (h + 1) * HD)


def text_step(q_ref, cases, text_k, text_v, bias):
    scores = [
        product(text_k[:, head_rows(h)], group_queries(q_ref, g, h)) * SCORE_SCALE + bias[...] for g, h in cases
    ]
    tops = [jnp.maximum(jnp.max(s, axis=0, keepdims=True), FLOOR) for s in scores]
    weights = [jnp.exp2(s - top) for s, top in zip(scores, tops)]
    totals = [jnp.sum(p, axis=0, keepdims=True) for p in weights]
    outs = [product(text_v[h], p.astype(jnp.bfloat16)) for (_, h), p in zip(cases, weights)]
    return list(zip(tops, totals, outs))


def group_cases(step, groups):
    return [(step * groups + j, h) for j in range(groups) for h in range(2)]


def joined(old, new):
    top = jnp.maximum(old[0], new[0])
    fade = jnp.exp2(old[0] - top)
    rise = jnp.exp2(new[0] - top)
    return top, old[1] * fade + new[1] * rise, old[2] * fade + new[2] * rise


def read_state(acc, stat, g, h):
    return stat[g, 2 * h : 2 * h + 1, :], stat[g, 2 * h + 1 : 2 * h + 2, :], acc[g, head_rows(h), :]


def write_state(acc, stat, g, h, state):
    stat[g, 2 * h : 2 * h + 1, :] = state[0]
    stat[g, 2 * h + 1 : 2 * h + 2, :] = state[1]
    acc[g, head_rows(h), :] = state[2]


def walk_units(units, count, q_ref, kv, acc, stat):
    def step(t, _):
        work = []
        for j in range(TOGETHER):
            number = t * TOGETHER + j
            code = jnp.where(number < count, units[number], 0)
            gone = jnp.where(number < count, 0.0, NEG)
            block = code >> 4
            g = block >> 1
            across = pl.multiple_of((block & 1) * BLK, BLK)
            who = (code & 15) >> 1
            down = pl.multiple_of((code & 1) * BLK, BLK)
            for h in range(2):
                s = product(
                    kv[who, pl.ds(down, BLK), head_rows(h)], q_ref[g, pl.ds(across, BLK), head_rows(h)]
                )
                work.append((g, across, who, down, h, gone, s * SCORE_SCALE))
        done = []
        for g, across, who, down, h, gone, s in work:
            top = jnp.max(s, axis=0, keepdims=True)
            p = jnp.exp2(s - top)
            total = jnp.sum(p, axis=0, keepdims=True)
            out = product(kv[who, pl.ds(down + 2 * BLK, BLK), head_rows(h)], p.astype(jnp.bfloat16))
            done.append((g, across, h, top + gone, total, out))
        for g, across, h, top, total, out in done:
            lanes = pl.ds(across, BLK)
            old_top = stat[g, 2 * h : 2 * h + 1, lanes]
            new_top = jnp.maximum(old_top, top)
            fade = jnp.exp2(old_top - new_top)
            rise = jnp.exp2(top - new_top)
            stat[g, 2 * h : 2 * h + 1, lanes] = new_top
            stat[g, 2 * h + 1 : 2 * h + 2, lanes] = (
                stat[g, 2 * h + 1 : 2 * h + 2, lanes] * fade + total * rise
            )
            acc[g, head_rows(h), lanes] = acc[g, head_rows(h), lanes] * fade + out * rise
        return 0

    lax.fori_loop(0, (count + TOGETHER - 1) // TOGETHER, step, 0)


def start_all(pairs, sems):
    copies = [pltpu.make_async_copy(src, dst, sems.at[i]) for i, (src, dst) in enumerate(pairs)]
    for copy in copies:
        copy.start()
    return [copy.wait for copy in copies]


def early_kernel(table, q_ref, own, f1, b1, f2, b2, acc, stat, kv, units, sems):
    waits = start_all([(x, kv.at[i]) for i, x in enumerate((own, f1, b1, f2, b2))], sems)
    count = list_units(table, 0, len(EARLY), units)
    for wait in waits[:3]:
        wait()
    offset = lax.broadcasted_iota(jnp.int32, (2 * BLK, 2 * BLK), 0) - lax.broadcasted_iota(
        jnp.int32, (2 * BLK, 2 * BLK), 1
    )
    distance = jnp.abs(offset)

    r = table[0, WHERE_AT + 1]
    for steps in ((0, 1), (2, 3), (4,)):
        cases = []
        for step in steps:
            g = (r + NEAR - step) & (ROW - 1)
            near = table[g, NEAR_AT]
            who = near & 15
            for h in range(2):
                s = product(kv[who, : 2 * BLK, head_rows(h)], group_queries(q_ref, g, h)) * SCORE_SCALE
                cases.append((g, h, who, jnp.where(distance < (near >> 4), s, NEG)))
        fresh = []
        for g, h, who, s in cases:
            top = jnp.maximum(jnp.max(s, axis=0, keepdims=True), FLOOR)
            p = jnp.exp2(s - top)
            values = jnp.concatenate(
                (kv[who, 2 * BLK : 3 * BLK, head_rows(h)], kv[who, 3 * BLK : 4 * BLK, head_rows(h)]), axis=1
            )
            out = product(values, p.astype(jnp.bfloat16))
            fresh.append((g, h, (top, jnp.sum(p, axis=0, keepdims=True), out)))
        for g, h, state in fresh:
            write_state(acc, stat, g, h, state)
            stat[g, 4:8, :] = jnp.zeros((4, 2 * BLK), jnp.float32)
    row = lax.broadcasted_iota(jnp.int32, (8, 2 * BLK), 0)
    for step in range(2 * NEAR + 1, ROW):
        g = (r + NEAR - step) & (ROW - 1)
        acc[g, :, :] = jnp.zeros((2 * HD, 2 * BLK), jnp.float32)
        stat[g, :, :] = jnp.where((row == 0) | (row == 2), FLOOR, 0.0)
    for wait in waits[3:]:
        wait()
    walk_units(units, count, q_ref, kv, acc, stat)


def late_kernel(
    table, q_ref, own, f1, b1, f2, b2, f3, b3, far4, acc_in, stat_in, out_ref, acc, stat,
    kv, units, sems, tiles, bias, text_k, text_v,
):
    pairs = [(f3, kv.at[0]), (b3, kv.at[1]), (far4, kv.at[2])]
    for i, x in enumerate((own, f1, b1, f2, b2, f3, b3, far4)):
        pairs.append((x.at[4 * BLK :], tiles.at[i]))
    waits = start_all(pairs, sems)
    count = list_units(table, len(EARLY), len(LATE), units)
    for wait in waits[3:]:
        wait()
    set_text(tiles, table, bias, text_k, text_v)
    for wait in waits[:3]:
        wait()
    walk_units(units, count, q_ref, kv, acc, stat)

    def some_groups(step, _):
        cases = group_cases(step, GROUPS_AT_ONCE)
        fresh = text_step(q_ref, cases, text_k, text_v, bias)
        done = [joined(read_state(acc, stat, g, h), new) for (g, h), new in zip(cases, fresh)]
        for x in range(0, len(cases), 2):
            g = cases[x][0]
            rows = []
            for h in range(2):
                top, total, out = done[x + h]
                out_ref[g, head_rows(h), :] = out.astype(jnp.bfloat16)
                rows += three_parts(top) + two_parts(total)
            rows.append(jnp.zeros((TPAD - len(rows), 2 * BLK), jnp.float32))
            out_ref[g, 2 * HD : 2 * HD + TPAD, :] = jnp.concatenate(rows, axis=0).astype(jnp.bfloat16)
        return 0

    lax.fori_loop(0, ROW // GROUPS_AT_ONCE, some_groups, 0)


def merge_kernel(part_ref, out_ref):
    stats = [part_ref[i, 2 * HD : 2 * HD + TPAD, :].astype(jnp.float32) for i in range(ROW)]
    for h in range(2):
        tops = [s[5 * h : 5 * h + 1] + s[5 * h + 1 : 5 * h + 2] + s[5 * h + 2 : 5 * h + 3] for s in stats]
        sums = [s[5 * h + 3 : 5 * h + 4] + s[5 * h + 4 : 5 * h + 5] for s in stats]
        top = functools.reduce(jnp.maximum, tops)
        weights = [jnp.exp2(t - top) for t in tops]
        total = functools.reduce(jnp.add, [w * s for w, s in zip(weights, sums)])
        inverse = 1.0 / total
        rows = slice(h * HD, (h + 1) * HD)
        acc = None
        for i in range(ROW):
            term = part_ref[i, rows, :].astype(jnp.float32) * weights[i]
            acc = term if acc is None else acc + term
        acc = (acc * inverse).astype(jnp.bfloat16)
        for i in range(ROW):
            out_ref[i, rows, :] = acc


def smem():
    return pl.BlockSpec(memory_space=pltpu.SMEM)


def vmem():
    return pl.BlockSpec(memory_space=pltpu.VMEM)


def anywhere():
    return pl.BlockSpec(memory_space=pl.ANY)


def kernel_params():
    return pltpu.CompilerParams(vmem_limit_bytes=32 << 20)


def attend_scratch(slots, copies):
    return [
        pltpu.VMEM((slots, MESSAGE, 2 * HD), jnp.bfloat16),
        pltpu.SMEM((2 * ROW * slots + 8,), jnp.int32),
        pltpu.SemaphoreType.DMA((copies,)),
    ]


def text_scratch():
    return [
        pltpu.VMEM((ROW, TPAD, 2 * HD), jnp.bfloat16),
        pltpu.VMEM((ROW * TEXT_ROWS, 2 * BLK), jnp.float32),
        pltpu.VMEM((ROW * TEXT_ROWS, 2 * HD), jnp.bfloat16),
        pltpu.VMEM((2, HD, ROW * TEXT_ROWS), jnp.bfloat16),
    ]


def shards(
    queries,
    keys,
    values,
    text_keys,
    text_values,
    text_len,
    radial_width,
    far_blocks,
    far_count,
    w_out,
):
    own = lax.axis_index("seq")
    where = jnp.stack((own // ROW, own % ROW, text_len[0])).astype(jnp.int32)
    tokens, width = queries.shape
    heads = lax.axis_size("head")
    columns = w_out.shape[1] // heads

    whole = pltpu.CompilerParams(vmem_limit_bytes=60 << 20)
    kv, q_mine = pl.pallas_call(
        message_kernel,
        out_shape=(
            jax.ShapeDtypeStruct((MESSAGE, width), jnp.bfloat16),
            jax.ShapeDtypeStruct((ROW, tokens, width), jnp.bfloat16),
        ),
        in_specs=[anywhere()] * 3 + [vmem()] * 2,
        out_specs=(vmem(), vmem()),
        scratch_shapes=[
            pltpu.VMEM((tokens, width), jnp.bfloat16),
            pltpu.VMEM((tokens, width), jnp.bfloat16),
            pltpu.SemaphoreType.DMA((3,)),
        ],
        compiler_params=whole,
        name="messages",
    )(keys, values, queries, text_keys, text_values)
    table, quarter = pl.pallas_call(
        list_kernel,
        out_shape=(
            jax.ShapeDtypeStruct((2 * ROW, BLK), jnp.int32),
            jax.ShapeDtypeStruct((heads, width // 4, columns), jnp.bfloat16),
        ),
        in_specs=[smem(), vmem(), vmem(), vmem(), anywhere()],
        out_specs=(vmem(), vmem()),
        scratch_shapes=[
            pltpu.VMEM((BLK, BLK), jnp.int32),
            pltpu.VMEM((BLK, BLK), jnp.int32),
            pltpu.SemaphoreType.DMA((heads,)),
        ],
        compiler_params=whole,
        cost_estimate=pl.CostEstimate(flops=40 * 10**9, bytes_accessed=10**5, transcendentals=0),
        name="lists",
    )(where, far_blocks.T, far_count[None, :], radial_width.T, w_out)

    count = ROW * ROW
    later, table = lax.optimization_barrier((kv, table))
    f1 = along_column(later, 1)
    b1 = along_column(later, -1)
    q_all = lax.all_to_all(q_mine, "seq", 0, 0, axis_index_groups=row_peers())
    f2 = along_column(kv, 2)
    b2 = along_column(kv, -2)
    f2, b2, table, quarter = lax.optimization_barrier((f2, b2, table, quarter))
    f3 = along_column(f2, 1)
    b3 = along_column(b2, -1)
    far4 = lax.ppermute(
        jnp.where(own % 2 == 0, f2, b2),
        "seq",
        [(g, (g + (2 * ROW if g % 2 == 0 else -2 * ROW)) % count) for g in range(count)],
    )
    quarter, q_all = lax.optimization_barrier((quarter, q_all))
    quarter = lax.all_to_all(quarter, "head", 0, 0)

    acc, stat = pl.pallas_call(
        early_kernel,
        out_shape=(
            jax.ShapeDtypeStruct((ROW, width, tokens), jnp.float32),
            jax.ShapeDtypeStruct((ROW, 8, tokens), jnp.float32),
        ),
        in_specs=[smem(), vmem()] + [anywhere()] * 5,
        out_specs=(vmem(), vmem()),
        scratch_shapes=attend_scratch(len(EARLY), 5),
        compiler_params=kernel_params(),
        cost_estimate=pl.CostEstimate(flops=6 * 10**9, bytes_accessed=5 * 10**6, transcendentals=0),
        name="attend_early",
    )(table, q_all, kv, f1, b1, f2, b2)
    part, _, _ = pl.pallas_call(
        late_kernel,
        out_shape=(
            jax.ShapeDtypeStruct((ROW, width + TPAD, tokens), jnp.bfloat16),
            jax.ShapeDtypeStruct(acc.shape, acc.dtype),
            jax.ShapeDtypeStruct(stat.shape, stat.dtype),
        ),
        in_specs=[smem(), vmem()] + [anywhere()] * 8 + [vmem()] * 2,
        out_specs=(vmem(),) * 3,
        scratch_shapes=attend_scratch(len(LATE), 3 + ROW) + text_scratch(),
        input_output_aliases={10: 1, 11: 2},
        compiler_params=kernel_params(),
        cost_estimate=pl.CostEstimate(flops=4 * 10**9, bytes_accessed=5 * 10**6, transcendentals=0),
        name="attend_late",
    )(table, q_all, kv, f1, b1, f2, b2, f3, b3, far4, acc, stat)
    part, quarter = lax.optimization_barrier((part, quarter))
    part = lax.all_to_all(part, "seq", 0, 0, axis_index_groups=row_peers())
    low = (own & ROW) == 0
    other = lax.ppermute(quarter, "seq", [(g, g ^ ROW) for g in range(count)])
    halves = jnp.stack((jnp.where(low, quarter, other), jnp.where(low, other, quarter)), axis=1)
    theirs = lax.ppermute(halves, "seq", [(g, g ^ 1) for g in range(count)])
    even = (own & 1) == 0
    w_mine = jnp.stack((jnp.where(even, halves, theirs), jnp.where(even, theirs, halves)), axis=2)
    merged = pl.pallas_call(
        merge_kernel,
        out_shape=jax.ShapeDtypeStruct((ROW, width, tokens), jnp.bfloat16),
        in_specs=[vmem()],
        out_specs=vmem(),
        compiler_params=kernel_params(),
        name="merge",
    )(part)
    attention = lax.all_to_all(merged, "head", 0, 0)
    mixed = lax.dot_general(
        attention.reshape(heads * width, tokens),
        w_mine.reshape(heads * width, columns),
        (((0,), (0,)), ((), ())),
        preferred_element_type=jnp.float32,
    )
    return mixed.astype(jnp.bfloat16)


def solution(mesh):
    return jax.shard_map(
        shards,
        mesh=mesh,
        in_specs=(
            P("seq", "head"),
            P("seq", "head"),
            P("seq", "head"),
            P("seq", "head"),
            P("seq", "head"),
            P(),
            P(),
            P(),
            P(),
            P("head", None),
        ),
        out_specs=P("seq", "head"),
        check_vma=False,
    )
```
